128 devices in a mesh: ctx: 32 (over x, z_lo, y), head: 4 (over z_hi, core).
Axes of the slice: x: 4, y: 4, z: 4 (z_hi: 2, z_lo: 2; z = z_hi * 2 + z_lo), core: 2. Of those that a mesh axis runs over, the one named last changes fastest.
Arguments:
- block_order: int32 [64], replicated, may hold values from 0 to 63, as said below
- query_latent: bfloat16 [4096, 128, 576], P('ctx', 'head'), may hold values from -12 to 12
- key_latent: bfloat16 [4096, 576], P('ctx'), may hold values from -6 to 6
- normalizer: float32 [4096, 128], P('ctx', 'head'), may hold values from 6 to 9
- indexer_query: bfloat16 [4096, 64, 128], P('ctx', 'head'), may hold values from -8 to 8
- indexer_key: bfloat16 [4096, 128], P('ctx'), may hold values from -4 to 4
- indexer_weight: bfloat16 [4096, 64], P('ctx', 'head'), may hold values from -4 to 4
Outputs:
- query_grad: float32 [4096, 64, 128], P('ctx', 'head')
- key_grad: float32 [4096, 128], P(('ctx', 'head'))
The draws below stay inside these ranges and needn't reach their ends.
Inputs may be any that keep to these rules, and one draw needn't show every extreme that they name: `block_order`: entries 2 i and 2 i + 1 are the blocks stored on ctx index i; all entries together are each of 0 to 63 once, and the two entries of one index sum to 63.
All inputs are finite; a program needn't handle non-finite values.
Results may differ from the reference program's by a relative error of at most 0.0037.
Values may be sent and summed in bfloat16 or wider, within the bound.
No kernel may reach another device: no remote copies, remote signals or barrier semaphores. Data moves between devices by JAX's collectives and lax.ppermute only.
A program may use at most 128 MiB of HBM per device.

```python
import math
import jax
import jax.numpy as jnp
from jax import lax

HEADS = 128
LATENT = 576
IDX_HEADS = 64
IDX_DIM = 128
HALF = 64
BLOCKS = 64
TOKENS = 4096


def scaled_rows(key, shape, lower, upper):
    return jnp.exp(jax.random.uniform(key, shape, jnp.float32, math.log(lower), math.log(upper)))


def draw_block_order(key, part):
    shuffled = jax.random.permutation(key, BLOCKS // 2).astype(jnp.int32)
    upper_block = BLOCKS - 1 - shuffled
    return jnp.stack((shuffled, upper_block), axis=1).reshape(-1).astype(jnp.int32)


def draw_query_latent(key, part):
    base_key = jax.random.fold_in(key, 21)
    scale_key = jax.random.fold_in(key, 22)
    row_scale = scaled_rows(scale_key, (TOKENS, HEADS, 1), 0.5, 4.0)
    values = jnp.clip(jax.random.normal(base_key, (TOKENS, HEADS, LATENT), jnp.float32), -3.0, 3.0)
    return (values * row_scale).astype(jnp.bfloat16)


def draw_key_latent(key, part):
    base_key = jax.random.fold_in(key, 23)
    scale_key = jax.random.fold_in(key, 24)
    row_scale = scaled_rows(scale_key, (TOKENS, 1), 0.5, 2.0)
    values = jnp.clip(jax.random.normal(base_key, (TOKENS, LATENT), jnp.float32), -3.0, 3.0)
    return (values * row_scale).astype(jnp.bfloat16)


def indexer_draw(key):
    query_key = jax.random.fold_in(key, 31)
    keyset_key = jax.random.fold_in(key, 32)
    weight_key = jax.random.fold_in(key, 33)
    query = jnp.clip(jax.random.normal(query_key, (TOKENS, IDX_HEADS, IDX_DIM), jnp.float32), -4.0, 4.0)
    keyset = jnp.clip(jax.random.normal(keyset_key, (TOKENS, IDX_DIM), jnp.float32), -4.0, 4.0)
    weight = jnp.clip(jax.random.normal(weight_key, (TOKENS, IDX_HEADS), jnp.float32), -4.0, 4.0)
    return (query, keyset, weight)


def draw_indexer_query(key, part):
    return indexer_draw(key)[0].astype(jnp.bfloat16)


def draw_indexer_key(key, part):
    return indexer_draw(key)[1].astype(jnp.bfloat16)


def draw_indexer_weight(key, part):
    return indexer_draw(key)[2].astype(jnp.bfloat16)


def shard_levels(stream_key, extent, split, least, top_value):
    def one(dim, shards_of):
        steps = jax.random.uniform(jax.random.fold_in(jax.random.fold_in(stream_key, 6), dim), (shards_of,), jnp.float32, least / len(split), top_value / len(split))
        return jnp.repeat(jnp.exp(steps), extent[dim] // shards_of).reshape((-1,) + (1,) * (len(extent) - dim - 1))

    factor_of = one(*split[0])
    for cut in split[1:]:
        factor_of = factor_of * one(*cut)
    return factor_of


def setup_inputs(seed: int = 0) -> dict:
    splits = jax.random.split(jax.random.key(seed), 8)
    block_order = draw_block_order(jax.random.fold_in(splits[7], 71), 0)
    query_latent = draw_query_latent(jax.random.fold_in(splits[7], 71), 0)
    key_latent = draw_key_latent(jax.random.fold_in(splits[7], 71), 0)
    normalizer = jnp.clip(6.0 + 3.0 * jax.random.uniform(splits[3], (TOKENS, HEADS), jnp.float32) ** shard_levels(splits[3], (TOKENS, HEADS), ((0, 32), (1, 4)), -0.2, 0.2), 6.0, 9.0)
    indexer_query = draw_indexer_query(jax.random.fold_in(splits[7], 71), 0)
    indexer_key = draw_indexer_key(jax.random.fold_in(splits[7], 71), 0)
    indexer_weight = draw_indexer_weight(jax.random.fold_in(splits[7], 71), 0)
    return {"block_order": block_order, "query_latent": query_latent, "key_latent": key_latent, "normalizer": normalizer, "indexer_query": indexer_query, "indexer_key": indexer_key, "indexer_weight": indexer_weight}


mla_scale = 192.0 ** -0.5
loss_scale = 64.0


def reference(block_order, query_latent, key_latent, normalizer, indexer_query, indexer_key, indexer_weight):
    query_rows = 2 * HALF
    block_count = TOKENS // query_rows
    positions = (block_order[:, None] * HALF + jnp.arange(HALF, dtype=jnp.int32)[None, :]).reshape(-1).astype(jnp.int32)
    kv_float = key_latent.astype(jnp.float32)
    key_float = indexer_key.astype(jnp.float32)
    idx_scale = (IDX_HEADS * IDX_DIM) ** -0.5

    def scan_step(key_accum, pieces):
        query_block, lse_block, idx_block, weight_block, query_pos = pieces
        scores = jnp.einsum('thl,sl->ths', query_block.astype(jnp.float32), kv_float) * mla_scale
        visible = positions[None, :] <= query_pos[:, None]
        target_sum = jnp.where(visible, jnp.sum(jnp.exp(scores - lse_block[:, :, None]), axis=1), 0.0)
        row_total = jnp.sum(target_sum, axis=1, keepdims=True)
        idx_dot = jnp.einsum('tjd,sd->tjs', idx_block.astype(jnp.float32), key_float)
        logits = idx_scale * jnp.sum(weight_block.astype(jnp.float32)[:, :, None] * jnp.maximum(idx_dot, 0.0), axis=1)
        row_top = jnp.max(jnp.where(visible, logits, -jnp.inf), axis=1, keepdims=True)
        exp_logit = jnp.where(visible, jnp.exp(logits - row_top), 0.0)
        norm_sum = jnp.sum(exp_logit, axis=1, keepdims=True)
        grad_logit = jnp.where(visible, loss_scale * (exp_logit / norm_sum - target_sum / row_total), 0.0).astype(jnp.bfloat16)
        weight_scaled = weight_block.astype(jnp.float32) * idx_scale
        coefficient = jnp.where(idx_dot > 0, grad_logit.astype(jnp.float32)[:, None, :] * weight_scaled[:, :, None], 0.0).astype(jnp.bfloat16)
        coeff_float = coefficient.astype(jnp.float32)
        query_part = jnp.einsum('tjs,sd->tjd', coeff_float, key_float)
        key_accum = key_accum + jnp.einsum('tjs,tjd->sd', coeff_float, idx_block.astype(jnp.float32))
        return key_accum, query_part

    pieces = (
        query_latent.reshape(block_count, query_rows, HEADS, LATENT),
        normalizer.reshape(block_count, query_rows, HEADS),
        indexer_query.reshape(block_count, query_rows, IDX_HEADS, IDX_DIM),
        indexer_weight.reshape(block_count, query_rows, IDX_HEADS),
        positions.reshape(block_count, query_rows),
    )
    key_grad, query_parts = lax.scan(scan_step, jnp.zeros((TOKENS, IDX_DIM), jnp.float32), pieces)
    query_grad = query_parts.reshape(TOKENS, IDX_HEADS, IDX_DIM)
    return query_grad, key_grad
```

```python
import functools
import math

import jax
import jax.numpy as jnp
from jax import lax
from jax.experimental import pallas as pl
from jax.experimental.pallas import tpu as pltpu
from jax.sharding import PartitionSpec as P

ALL = ("ctx", "head")
HALF = 64
TILE = 256
PER_TILE = TILE // HALF
TILES = 17
MLA_SCALE = 192.0**-0.5
LOSS_SCALE = 64.0
NT = (((1,), (1,)), ((), ()))
NN = (((1,), (0,)), ((), ()))


def permutation(move):
    pairs = []
    for x in range(4):
        for zl in range(2):
            for y in range(4):
                for zh in range(2):
                    for k in range(2):
                        tx, tz, ty, tk = move(x, 2 * zh + zl, y, k)
                        tx, tz, ty, tk = tx % 4, tz % 4, ty % 4, tk % 2
                        source = (x * 8 + zl * 4 + y) * 4 + zh * 2 + k
                        target = (tx * 8 + (tz % 2) * 4 + ty) * 4 + (tz // 2) * 2 + tk
                        pairs.append((source, target))
    return pairs


def send(value, move):
    return lax.ppermute(value, ALL, permutation(move))


def swap_core(value):
    return send(value, lambda x, z, y, k: (x, z, y, k + 1))


def swap_high(value):
    return send(value, lambda x, z, y, k: (x, z + 2, y, k))


def along(first, shift):
    def move(x, z, y, k):
        if (k == 0) == first:
            return (x, z, y + shift, k)
        return (x + shift, z, y, k)

    return move


def vmem():
    return pl.BlockSpec(memory_space=pltpu.VMEM)


def smem():
    return pl.BlockSpec(memory_space=pltpu.SMEM)


def anywhere():
    return pl.BlockSpec(memory_space=pl.ANY)


def params(mib):
    return pltpu.CompilerParams(vmem_limit_bytes=mib * 1024 * 1024)


def place(meta, step):
    half = (step >= meta[0]).astype(jnp.int32)
    return half, step - half * meta[0]


def target_kernel(meta, loc, q_ref, m0, m1, m2, m3, s0, s1, s2, s3, keep, other, sorted_ref, keys, sems):
    core = meta[1]
    copies = []
    for side, group in enumerate(((m0, m1, m2, m3), (s0, s1, s2, s3))):
        owner = core if side == 0 else 1 - core
        for j, ref in enumerate(group):
            copies.append(
                pltpu.make_async_copy(ref, keys.at[pl.ds(owner * 32 + j * 8, 8)], sems.at[side * 4 + j])
            )
    for copy in copies:
        copy.start()
    for copy in copies:
        copy.wait()

    def sort(p, _):
        sorted_ref[pl.ds(pl.multiple_of(p * HALF, HALF), HALF), :] = keys[loc[p], :, 640:768]
        return 0

    lax.fori_loop(0, 64, sort, 0, unroll=4)
    scale = MLA_SCALE * math.log2(math.e)

    def body(step, _):
        half, ktile = place(meta, step)
        tile = jnp.concatenate(
            [keys[loc[ktile * PER_TILE + u], :, 0:640] for u in range(PER_TILE)], axis=0
        )
        total = jnp.zeros((HALF, TILE), jnp.float32)
        for g in range(8):
            rows = q_ref[pl.ds(pl.multiple_of(half * 2048 + g * 256, 256), 256), :]
            s = lax.dot_general(rows, tile, NT, preferred_element_type=jnp.float32)
            e = jnp.exp2(s * scale)
            total = total + ((e[0:64] + e[64:128]) + (e[128:192] + e[192:256]))
        top, low = total[0:32], total[32:64]
        keep[step] = jnp.where(core == 0, top, low)
        other[step] = jnp.where(core == 0, low, top)
        return 0

    lax.fori_loop(0, TILES, body, 0)


def visible_of(meta, half, ktile):
    rows = lax.broadcasted_iota(jnp.int32, (32, TILE), 0) + meta[1] * 32 + meta[2 + half] * HALF
    cols = lax.broadcasted_iota(jnp.int32, (32, TILE), 1) + ktile * TILE
    return cols <= rows


def logit_kernel(idx_scale, meta, a_ref, b_ref, key_ref, out, wide, top, norm):
    for side, ref in enumerate((a_ref, b_ref)):
        for c in range(2):
            for half in range(2):
                w = ref[c, half, 16].astype(jnp.float32)
                for j in range(16):
                    wide[side, c, half, pl.ds(j * 32, 32)] = jnp.broadcast_to(w[:, j : j + 1], (32, 128))
    top[...] = jnp.full(top.shape, -jnp.inf, jnp.float32)
    norm[...] = jnp.zeros(norm.shape, jnp.float32)

    def first(step, _):
        half, ktile = place(meta, step)
        tile = key_ref[pl.ds(pl.multiple_of(ktile * TILE, TILE), TILE), :]
        total = jnp.zeros((32, TILE), jnp.float32)
        for side, ref in enumerate((a_ref, b_ref)):
            for c in range(2):
                rows = ref[c, half, 0:16].reshape(512, 128)
                d = jnp.maximum(lax.dot_general(rows, tile, NT, preferred_element_type=jnp.float32), 0.0)
                w = wide[side, c, half]
                d = d * jnp.concatenate((w, w), axis=1)
                for j in range(16):
                    total = total + d[j * 32 : (j + 1) * 32]
        logits = jnp.where(visible_of(meta, half, ktile), total * idx_scale, -jnp.inf)
        out[step] = logits
        top[half] = jnp.maximum(top[half], logits)
        return 0

    lax.fori_loop(0, TILES, first, 0)
    for half in range(2):
        top[half] = jnp.broadcast_to(jnp.max(top[half], axis=1, keepdims=True), (32, TILE))

    def second(step, _):
        half, _ktile = place(meta, step)
        e = jnp.exp(out[step] - top[half])
        out[step] = e
        norm[half] = norm[half] + e
        return 0

    lax.fori_loop(0, TILES, second, 0)
    for half in range(2):
        norm[half] = jnp.broadcast_to(1.0 / jnp.sum(norm[half], axis=1, keepdims=True), (32, TILE))

    def third(step, _):
        half, _ktile = place(meta, step)
        out[step] = out[step] * norm[half]
        return 0

    lax.fori_loop(0, TILES, third, 0)


def gradient_kernel(meta, p_ref, a_ref, b_ref, c_ref, out, whole, total):
    total[...] = jnp.zeros(total.shape, jnp.float32)

    def first(step, _):
        half, ktile = place(meta, step)
        t = a_ref[step] + b_ref[step] + c_ref[step].astype(jnp.float32)
        t = jnp.where(visible_of(meta, half, ktile), t, 0.0)
        whole[step] = t
        total[half] = total[half] + t
        return 0

    lax.fori_loop(0, TILES, first, 0)
    for half in range(2):
        total[half] = jnp.broadcast_to(1.0 / jnp.sum(total[half], axis=1, keepdims=True), (32, TILE))

    def second(step, _):
        half, _ktile = place(meta, step)
        out[step] = (LOSS_SCALE * (p_ref[step] - whole[step] * total[half])).astype(jnp.bfloat16)
        return 0

    lax.fori_loop(0, TILES, second, 0)


def backward_kernel(
    idx_scale, meta, stored, g_ref, h_ref, iq_ref, iqt_ref, key_ref, dq, keep, other, wide
):
    core = meta[1]
    for half in range(2):
        w = iq_ref[half, 16].astype(jnp.float32) * idx_scale
        for j in range(16):
            wide[half, pl.ds(j * HALF, HALF)] = jnp.broadcast_to(w[:, j : j + 1], (HALF, 128))
    dq[...] = jnp.zeros(dq.shape, jnp.float32)
    keep[...] = jnp.zeros(keep.shape, jnp.float32)
    other[...] = jnp.zeros(other.shape, jnp.float32)

    def body(step, _):
        half, ktile = place(meta, step)
        tile = key_ref[pl.ds(pl.multiple_of(ktile * TILE, TILE), TILE), :]
        mine, theirs = g_ref[step].astype(jnp.float32), h_ref[step].astype(jnp.float32)
        g = jnp.concatenate(
            (jnp.where(core == 0, mine, theirs), jnp.where(core == 0, theirs, mine)), axis=0
        )
        g = jnp.concatenate((g, g, g, g), axis=0)
        dkt = jnp.zeros((128, TILE), jnp.float32)
        for q in range(4):
            rows = iq_ref[half, pl.ds(q * 4, 4)].reshape(256, 128)
            d = lax.dot_general(rows, tile, NT, preferred_element_type=jnp.float32)
            w = wide[half, pl.ds(q * 256, 256)]
            coefficient = jnp.where(d > 0, g * jnp.concatenate((w, w), axis=1), 0.0).astype(jnp.bfloat16)
            dq[half, pl.ds(q * 256, 256)] = dq[half, pl.ds(q * 256, 256)] + lax.dot_general(
                coefficient, tile, NN, preferred_element_type=jnp.float32
            )
            dkt = dkt + lax.dot_general(
                iqt_ref[half, :, q * 256 : (q + 1) * 256], coefficient, NN, preferred_element_type=jnp.float32
            )
        dk = dkt.T
        for u in range(PER_TILE):
            slot, slot_other = stored[ktile * PER_TILE + u], stored[64 + ktile * PER_TILE + u]
            first, last = dk[u * 64 : u * 64 + 32], dk[u * 64 + 32 : u * 64 + 64]
            keep[slot] = keep[slot] + jnp.where(core == 0, first, last)
            other[slot_other] = other[slot_other] + jnp.where(core == 0, last, first)
        return 0

    lax.fori_loop(0, TILES, body, 0)


def ring_sum(value, route):
    got = [send(value[shift], route(shift)) for shift in (1, 3, 2)]
    return value[0] + got[0] + got[1] + got[2]


def per_device(
    block_order, query_latent, key_latent, normalizer, indexer_query, indexer_key, indexer_weight
):
    f32, bf16 = jnp.float32, jnp.bfloat16
    idx_scale = 8192.0**-0.5
    ctx, head = lax.axis_index("ctx"), lax.axis_index("head")
    x, zl, y = ctx // 8, (ctx // 4) % 2, ctx % 4
    core = head % 2

    ones = (lax.broadcasted_iota(jnp.int32, (128, 64), 1) < 3).astype(bf16)
    packed = jnp.concatenate((key_latent, ones, indexer_key), axis=1)
    own = lax.dynamic_slice_in_dim(packed, core * HALF, HALF, 0)
    beside = send(own, lambda x, z, y, k: (x, z + 1 - 2 * k, y, k))
    pair = jnp.stack((own, beside))
    legs = [pair] + [send(pair, along(True, shift)) for shift in (1, 3, 2)]
    group = jnp.concatenate(legs, axis=0)
    up, down = send(group, along(False, 1)), send(group, along(False, 3))
    far_a = send(up[0:4], along(False, 1))
    far_b = send(down[4:8], along(False, 3))
    far = jnp.concatenate((far_a, far_b), axis=0)
    mine = [group, up, down, far]
    swapped = [swap_core(v) for v in mine]

    index = jnp.arange(64, dtype=jnp.int32)
    bc, bk = index // 2, index % 2
    bx, bz, by = bc // 8, (bc // 4) % 2, bc % 4

    def ring_slot(rel):
        return jnp.where(rel == 0, 0, jnp.where(rel == 3, 1, jnp.where(rel == 1, 2, 3)))

    rx, ry = ring_slot((bx - x) % 4), ring_slot((by - y) % 4)
    rz = (bz != zl).astype(jnp.int32)
    slot = bk * 32 + jnp.where(bk == 0, rx * 8 + ry * 2, ry * 8 + rx * 2) + rz
    hit = (block_order[None, :] == index[:, None]).astype(jnp.int32)
    loc = jnp.sum(hit * slot[None, :], axis=1)
    blocks = lax.dynamic_slice_in_dim(block_order, ctx * 2, 2, 0)
    qx, qy = (bx - x) % 4, (by - y) % 4
    qz = (2 * bk + bz - 2 * (head // 2) - zl) % 4
    row_a, row_b = qy * 16 + qx * 4 + qz, qx * 16 + qy * 4 + qz
    row_a, row_b = jnp.where(core == 0, row_a, row_b), jnp.where(core == 0, row_b, row_a)
    stored = jnp.concatenate((jnp.sum(hit * row_a[None, :], axis=1), jnp.sum(hit * row_b[None, :], axis=1)))
    meta = jnp.concatenate(((blocks[0:1] + PER_TILE) // PER_TILE, core[None], blocks)).astype(jnp.int32)

    lifted = -normalizer * math.sqrt(192.0)
    n1 = lax.reduce_precision(lifted, 8, 7)
    n2 = lax.reduce_precision(lifted - n1, 8, 7)
    n3 = lax.reduce_precision(lifted - n1 - n2, 8, 7)
    columns = jnp.stack((n1, n2, n3), axis=-1).astype(bf16)
    columns = jnp.pad(columns, ((0, 0), (0, 0), (0, 61)))
    query = jnp.concatenate((query_latent, columns), axis=2)
    query = query.reshape(2, HALF, 32, 640).transpose(0, 2, 1, 3).reshape(4096, 640)

    iq = indexer_query.reshape(2, HALF, 16, 128).transpose(0, 2, 1, 3)
    weight = jnp.pad(indexer_weight.reshape(2, 1, HALF, 16), ((0, 0), (0, 0), (0, 0), (0, 112)))
    iqw = jnp.concatenate((iq, weight), axis=1)
    iqt = iq.transpose(0, 3, 1, 2).reshape(2, 128, 1024)
    iq_keep = lax.dynamic_slice_in_dim(iqw, core * 32, 32, 2)
    iq_other = swap_core(lax.dynamic_slice_in_dim(iqw, (1 - core) * 32, 32, 2))
    iq_chip = jnp.stack((iq_keep, iq_other))
    iq_far = swap_high(iq_chip)

    part = jax.ShapeDtypeStruct((TILES, 32, TILE), f32)
    keep, other, sorted_keys = pl.pallas_call(
        target_kernel,
        out_shape=(part, part, jax.ShapeDtypeStruct((4096, 128), bf16)),
        in_specs=[smem(), smem(), vmem()] + [anywhere()] * 8,
        out_specs=(vmem(), vmem(), vmem()),
        scratch_shapes=[pltpu.VMEM((64, HALF, 768), bf16), pltpu.SemaphoreType.DMA((8,))],
        compiler_params=params(40),
        cost_estimate=pl.CostEstimate(flops=12_000_000_000, bytes_accessed=14_000_000, transcendentals=9_000_000),
        name="targets",
    )(meta, loc, query, *mine, *swapped)

    from_core = swap_core(other)
    from_high = swap_high((keep + from_core).astype(bf16))

    prob = pl.pallas_call(
        functools.partial(logit_kernel, idx_scale),
        out_shape=part,
        in_specs=[smem(), vmem(), vmem(), vmem()],
        out_specs=vmem(),
        scratch_shapes=[
            pltpu.VMEM((2, 2, 2, 512, 128), f32),
            pltpu.VMEM((2, 32, TILE), f32),
            pltpu.VMEM((2, 32, TILE), f32),
        ],
        compiler_params=params(24),
        cost_estimate=pl.CostEstimate(flops=5_000_000_000, bytes_accessed=4_000_000, transcendentals=200_000),
        name="logits",
    )(meta, iq_chip, iq_far, sorted_keys)

    grad = pl.pallas_call(
        gradient_kernel,
        out_shape=jax.ShapeDtypeStruct((TILES, 32, TILE), bf16),
        in_specs=[smem()] + [vmem()] * 4,
        out_specs=vmem(),
        scratch_shapes=[pltpu.VMEM((TILES, 32, TILE), f32), pltpu.VMEM((2, 32, TILE), f32)],
        compiler_params=params(16),
        name="gradient",
    )(meta, prob, keep, from_core, from_high)
    grad_other = swap_core(grad)

    shard = jax.ShapeDtypeStruct((64, 32, 128), f32)
    dq, dk_keep, dk_other = pl.pallas_call(
        functools.partial(backward_kernel, idx_scale),
        out_shape=(jax.ShapeDtypeStruct((2, 1024, 128), f32), shard, shard),
        in_specs=[smem(), smem()] + [vmem()] * 5,
        out_specs=(vmem(), vmem(), vmem()),
        scratch_shapes=[pltpu.VMEM((2, 1024, 128), f32)],
        compiler_params=params(24),
        name="backward",
    )(meta, stored, grad, grad_other, iqw, iqt, sorted_keys)

    query_grad = dq.reshape(2, 16, HALF, 128).transpose(0, 2, 1, 3).reshape(128, 16, 128)

    dk = dk_keep + swap_core(dk_other)
    dk = ring_sum(dk.reshape(4, 4, 4, 32, 128), functools.partial(along, True))
    dk = ring_sum(dk, functools.partial(along, False))
    dk = ring_sum(dk, lambda shift: lambda x, z, y, k: (x, z + shift, y, k))
    return query_grad, dk


def solution(mesh):
    return jax.shard_map(
        per_device,
        mesh=mesh,
        in_specs=(
            P(),
            P("ctx", "head", None),
            P("ctx", None),
            P("ctx", "head"),
            P("ctx", "head", None),
            P("ctx", None),
            P("ctx", "head"),
        ),
        out_specs=(P("ctx", "head", None), P(("ctx", "head"), None)),
        check_vma=False,
    )
```

```python
import functools
import math

import jax
import jax.numpy as jnp
from jax import lax
from jax.experimental import pallas as pl
from jax.experimental.pallas import tpu as pltpu
from jax.sharding import PartitionSpec as P

ALL = ("ctx", "head")
HALF = 64
TILE = 256
PER_TILE = TILE // HALF
TILES = 17
MLA_SCALE = 192.0**-0.5
LOSS_SCALE = 64.0
NT = (((1,), (1,)), ((), ()))
NN = (((1,), (0,)), ((), ()))


def permutation(move):
    pairs = []
    for x in range(4):
        for zl in range(2):
            for y in range(4):
                for zh in range(2):
                    for k in range(2):
                        tx, tz, ty, tk = move(x, 2 * zh + zl, y, k)
                        tx, tz, ty, tk = tx % 4, tz % 4, ty % 4, tk % 2
                        source = (x * 8 + zl * 4 + y) * 4 + zh * 2 + k
                        target = (tx * 8 + (tz % 2) * 4 + ty) * 4 + (tz // 2) * 2 + tk
                        pairs.append((source, target))
    return pairs


def send(value, move):
    return lax.ppermute(value, ALL, permutation(move))


def swap_core(value):
    return send(value, lambda x, z, y, k: (x, z, y, k + 1))


def swap_high(value):
    return send(value, lambda x, z, y, k: (x, z + 2, y, k))


def along(first, shift):
    def move(x, z, y, k):
        if (k == 0) == first:
            return (x, z, y + shift, k)
        return (x + shift, z, y, k)

    return move


def vmem():
    return pl.BlockSpec(memory_space=pltpu.VMEM)


def smem():
    return pl.BlockSpec(memory_space=pltpu.SMEM)


def anywhere():
    return pl.BlockSpec(memory_space=pl.ANY)


def params(mib):
    return pltpu.CompilerParams(vmem_limit_bytes=mib * 1024 * 1024)


def place(meta, step):
    half = (step >= meta[0]).astype(jnp.int32)
    return half, step - half * meta[0]


def pack_kernel(q_ref, n_ref, out):
    n = n_ref[...] * -math.sqrt(192.0)
    n1 = n.astype(jnp.bfloat16).astype(jnp.float32)
    n2 = (n - n1).astype(jnp.bfloat16).astype(jnp.float32)
    n3 = n - n1 - n2
    row = lax.broadcasted_iota(jnp.int32, (64, 128), 0)
    for i in range(16):
        lanes = slice(i * 128, (i + 1) * 128)
        a, b = q_ref[2 * i], q_ref[2 * i + 1]
        out[0, 0:576, lanes] = jnp.concatenate((a[:, 0:64], b[:, 0:64]), axis=1)
        out[1, 0:576, lanes] = jnp.concatenate((a[:, 64:128], b[:, 64:128]), axis=1)
        for half in range(2):
            cut = slice(half * 64, half * 64 + 64)
            parts = [
                jnp.concatenate((v[2 * i : 2 * i + 1, cut], v[2 * i + 1 : 2 * i + 2, cut]), axis=1)
                for v in (n1, n2, n3)
            ]
            block = jnp.where(row == 0, parts[0], jnp.where(row == 1, parts[1], jnp.where(row == 2, parts[2], 0.0)))
            out[half, 576:640, lanes] = block.astype(jnp.bfloat16)


def target_kernel(meta, loc, q_ref, m0, m1, m2, m3, s0, s1, s2, s3, keep, other, sorted_ref, keys, sems):
    core = meta[1]
    copies = []
    for side, group in enumerate(((m0, m1, m2, m3), (s0, s1, s2, s3))):
        owner = core if side == 0 else 1 - core
        for j, ref in enumerate(group):
            copies.append(
                pltpu.make_async_copy(ref, keys.at[pl.ds(owner * 32 + j * 8, 8)], sems.at[side * 4 + j])
            )
    for copy in copies:
        copy.start()
    for copy in copies:
        copy.wait()

    def sort(p, _):
        sorted_ref[pl.ds(pl.multiple_of(p * HALF, HALF), HALF), :] = keys[loc[p], :, 640:768]
        return 0

    lax.fori_loop(0, 64, sort, 0, unroll=4)
    scale = MLA_SCALE * math.log2(math.e)

    def body(step, _):
        half, ktile = place(meta, step)
        tile = jnp.concatenate(
            [keys[loc[ktile * PER_TILE + u], :, 0:640] for u in range(PER_TILE)], axis=0
        )
        total = jnp.zeros((TILE, 128), jnp.float32)
        for g in range(8):
            s = lax.dot_general(
                tile, q_ref[half, :, g * 256 : (g + 1) * 256], NN, preferred_element_type=jnp.float32
            )
            e = jnp.exp2(s * scale)
            total = total + (e[:, 0:128] + e[:, 128:256])
        total = total.T
        total = total[0:64] + total[64:128]
        top, low = total[0:32], total[32:64]
        keep[step] = jnp.where(core == 0, top, low)
        other[step] = jnp.where(core == 0, low, top)
        return 0

    lax.fori_loop(0, TILES, body, 0, unroll=4)


def visible_of(meta, half, ktile):
    rows = lax.broadcasted_iota(jnp.int32, (32, TILE), 0) + meta[1] * 32 + meta[2 + half] * HALF
    cols = lax.broadcasted_iota(jnp.int32, (32, TILE), 1) + ktile * TILE
    return cols <= rows


def logit_kernel(idx_scale, meta, a_ref, b_ref, key_ref, out, wide, top, norm):
    for side, ref in enumerate((a_ref, b_ref)):
        for c in range(2):
            for half in range(2):
                w = ref[c, half, 16].astype(jnp.float32)
                for j in range(16):
                    wide[side, c, half, pl.ds(j * 32, 32)] = jnp.broadcast_to(w[:, j : j + 1], (32, 128))
    top[...] = jnp.full(top.shape, -jnp.inf, jnp.float32)
    norm[...] = jnp.zeros(norm.shape, jnp.float32)

    def first(step, _):
        half, ktile = place(meta, step)
        tile = key_ref[pl.ds(pl.multiple_of(ktile * TILE, TILE), TILE), :]
        total = jnp.zeros((32, TILE), jnp.float32)
        for side, ref in enumerate((a_ref, b_ref)):
            for c in range(2):
                rows = ref[c, half, 0:16].reshape(512, 128)
                d = jnp.maximum(lax.dot_general(rows, tile, NT, preferred_element_type=jnp.float32), 0.0)
                w = wide[side, c, half]
                d = d * jnp.concatenate((w, w), axis=1)
                for j in range(16):
                    total = total + d[j * 32 : (j + 1) * 32]
        logits = jnp.where(visible_of(meta, half, ktile), total * idx_scale, -jnp.inf)
        out[step] = logits
        top[half] = jnp.maximum(top[half], logits)
        return 0

    lax.fori_loop(0, TILES, first, 0, unroll=4)
    for half in range(2):
        top[half] = jnp.broadcast_to(jnp.max(top[half], axis=1, keepdims=True), (32, TILE))

    def second(step, _):
        half, _ktile = place(meta, step)
        e = jnp.exp(out[step] - top[half])
        out[step] = e
        norm[half] = norm[half] + e
        return 0

    lax.fori_loop(0, TILES, second, 0)
    for half in range(2):
        norm[half] = jnp.broadcast_to(1.0 / jnp.sum(norm[half], axis=1, keepdims=True), (32, TILE))

    def third(step, _):
        half, _ktile = place(meta, step)
        out[step] = out[step] * norm[half]
        return 0

    lax.fori_loop(0, TILES, third, 0)


def gradient_kernel(meta, p_ref, a_ref, b_ref, c_ref, out, whole, total):
    total[...] = jnp.zeros(total.shape, jnp.float32)

    def first(step, _):
        half, ktile = place(meta, step)
        t = a_ref[step] + b_ref[step] + c_ref[step].astype(jnp.float32)
        t = jnp.where(visible_of(meta, half, ktile), t, 0.0)
        whole[step] = t
        total[half] = total[half] + t
        return 0

    lax.fori_loop(0, TILES, first, 0)
    for half in range(2):
        total[half] = jnp.broadcast_to(1.0 / jnp.sum(total[half], axis=1, keepdims=True), (32, TILE))

    def second(step, _):
        half, _ktile = place(meta, step)
        out[step] = (LOSS_SCALE * (p_ref[step] - whole[step] * total[half])).astype(jnp.bfloat16)
        return 0

    lax.fori_loop(0, TILES, second, 0)


def spread(iq_ref, wide, idx_scale):
    for half in range(2):
        w = iq_ref[half, 16].astype(jnp.float32) * idx_scale
        for j in range(16):
            wide[half, pl.ds(j * HALF, HALF)] = jnp.broadcast_to(w[:, j : j + 1], (HALF, 128))


def coefficients(meta, step, g_ref, h_ref, iq_ref, key_ref, wide):
    core = meta[1]
    half, ktile = place(meta, step)
    tile = key_ref[pl.ds(pl.multiple_of(ktile * TILE, TILE), TILE), :]
    mine, theirs = g_ref[step].astype(jnp.float32), h_ref[step].astype(jnp.float32)
    g = jnp.concatenate((jnp.where(core == 0, mine, theirs), jnp.where(core == 0, theirs, mine)), axis=0)
    g = jnp.concatenate((g, g, g, g), axis=0)
    found = []
    for q in range(4):
        rows = iq_ref[half, pl.ds(q * 4, 4)].reshape(256, 128)
        d = lax.dot_general(rows, tile, NT, preferred_element_type=jnp.float32)
        w = wide[half, pl.ds(q * 256, 256)]
        found.append(jnp.where(d > 0, g * jnp.concatenate((w, w), axis=1), 0.0).astype(jnp.bfloat16))
    return half, ktile, tile, found


def key_kernel(idx_scale, meta, stored, g_ref, h_ref, iq_ref, iqt_ref, key_ref, keep, other, wide):
    core = meta[1]
    spread(iq_ref, wide, idx_scale)
    keep[...] = jnp.zeros(keep.shape, jnp.float32)
    other[...] = jnp.zeros(other.shape, jnp.float32)

    def body(step, _):
        half, ktile, _tile, found = coefficients(meta, step, g_ref, h_ref, iq_ref, key_ref, wide)
        dkt = lax.dot_general(
            iqt_ref[half], jnp.concatenate(found, axis=0), NN, preferred_element_type=jnp.float32
        )
        dk = dkt.T
        for u in range(PER_TILE):
            slot, slot_other = stored[ktile * PER_TILE + u], stored[64 + ktile * PER_TILE + u]
            first, last = dk[u * 64 : u * 64 + 32], dk[u * 64 + 32 : u * 64 + 64]
            keep[slot] = keep[slot] + jnp.where(core == 0, first, last)
            other[slot_other] = other[slot_other] + jnp.where(core == 0, last, first)
        return 0

    lax.fori_loop(0, TILES, body, 0, unroll=4)


def query_kernel(idx_scale, meta, g_ref, h_ref, iq_ref, key_ref, dq, wide):
    spread(iq_ref, wide, idx_scale)
    dq[...] = jnp.zeros(dq.shape, jnp.float32)

    def body(step, _):
        half, _ktile, tile, found = coefficients(meta, step, g_ref, h_ref, iq_ref, key_ref, wide)
        for q in range(4):
            dq[half, pl.ds(q * 256, 256)] = dq[half, pl.ds(q * 256, 256)] + lax.dot_general(
                found[q], tile, NN, preferred_element_type=jnp.float32
            )
        return 0

    lax.fori_loop(0, TILES, body, 0, unroll=4)


def ring_sum(value, route):
    got = [send(value[shift], route(shift)) for shift in (1, 3, 2)]
    return value[0] + got[0] + got[1] + got[2]


def per_device(
    block_order, query_latent, key_latent, normalizer, indexer_query, indexer_key, indexer_weight
):
    f32, bf16 = jnp.float32, jnp.bfloat16
    idx_scale = 8192.0**-0.5
    ctx, head = lax.axis_index("ctx"), lax.axis_index("head")
    x, zl, y = ctx // 8, (ctx // 4) % 2, ctx % 4
    core = head % 2

    ones = (lax.broadcasted_iota(jnp.int32, (128, 64), 1) < 3).astype(bf16)
    packed = jnp.concatenate((key_latent, ones, indexer_key), axis=1)
    own = lax.dynamic_slice_in_dim(packed, core * HALF, HALF, 0)
    beside = send(own, lambda x, z, y, k: (x, z + 1 - 2 * k, y, k))
    pair = jnp.stack((own, beside))
    legs = [pair] + [send(pair, along(True, shift)) for shift in (1, 3, 2)]
    group = jnp.concatenate(legs, axis=0)
    query = pl.pallas_call(
        pack_kernel,
        out_shape=jax.ShapeDtypeStruct((2, 640, 2048), bf16),
        in_specs=[vmem(), vmem()],
        out_specs=vmem(),
        compiler_params=params(8),
        cost_estimate=pl.CostEstimate(flops=0, bytes_accessed=12_000_000, transcendentals=0),
        name="pack",
    )(query_latent.transpose(1, 2, 0), normalizer.T)

    iq = indexer_query.reshape(2, HALF, 16, 128).transpose(0, 2, 1, 3)
    weight = jnp.pad(indexer_weight.reshape(2, 1, HALF, 16), ((0, 0), (0, 0), (0, 0), (0, 112)))
    iqw = jnp.concatenate((iq, weight), axis=1)
    iqt = iq.transpose(0, 3, 1, 2).reshape(2, 128, 1024)
    iq_keep = lax.dynamic_slice_in_dim(iqw, core * 32, 32, 2)
    iq_other = swap_core(lax.dynamic_slice_in_dim(iqw, (1 - core) * 32, 32, 2))
    iq_chip = jnp.stack((iq_keep, iq_other))
    group, iq_chip = lax.optimization_barrier((group, iq_chip))
    iq_far = swap_high(iq_chip)

    up, down = send(group, along(False, 1)), send(group, along(False, 3))
    up, query = lax.optimization_barrier((up, query))
    far_a = send(up[0:4], along(False, 1))
    far_b = send(down[4:8], along(False, 3))
    far = jnp.concatenate((far_a, far_b), axis=0)
    far, iq_far, iqt = lax.optimization_barrier((far, iq_far, iqt))
    mine = [group, up, down, far]
    swapped = [swap_core(v) for v in mine]

    index = jnp.arange(64, dtype=jnp.int32)
    bc, bk = index // 2, index % 2
    bx, bz, by = bc // 8, (bc // 4) % 2, bc % 4

    def ring_slot(rel):
        return jnp.where(rel == 0, 0, jnp.where(rel == 3, 1, jnp.where(rel == 1, 2, 3)))

    rx, ry = ring_slot((bx - x) % 4), ring_slot((by - y) % 4)
    rz = (bz != zl).astype(jnp.int32)
    slot = bk * 32 + jnp.where(bk == 0, rx * 8 + ry * 2, ry * 8 + rx * 2) + rz
    hit = (block_order[None, :] == index[:, None]).astype(jnp.int32)
    loc = jnp.sum(hit * slot[None, :], axis=1)
    blocks = lax.dynamic_slice_in_dim(block_order, ctx * 2, 2, 0)
    qx, qy = (bx - x) % 4, (by - y) % 4
    qz = (2 * bk + bz - 2 * (head // 2) - zl) % 4
    row_a, row_b = qy * 16 + qx * 4 + qz, qx * 16 + qy * 4 + qz
    row_a, row_b = jnp.where(core == 0, row_a, row_b), jnp.where(core == 0, row_b, row_a)
    stored = jnp.concatenate((jnp.sum(hit * row_a[None, :], axis=1), jnp.sum(hit * row_b[None, :], axis=1)))
    meta = jnp.concatenate(((blocks[0:1] + PER_TILE) // PER_TILE, core[None], blocks)).astype(jnp.int32)

    part = jax.ShapeDtypeStruct((TILES, 32, TILE), f32)
    keep, other, sorted_keys = pl.pallas_call(
        target_kernel,
        out_shape=(part, part, jax.ShapeDtypeStruct((4096, 128), bf16)),
        in_specs=[smem(), smem(), vmem()] + [anywhere()] * 8,
        out_specs=(vmem(), vmem(), vmem()),
        scratch_shapes=[pltpu.VMEM((64, HALF, 768), bf16), pltpu.SemaphoreType.DMA((8,))],
        compiler_params=params(16),
        cost_estimate=pl.CostEstimate(flops=12_000_000_000, bytes_accessed=14_000_000, transcendentals=9_000_000),
        name="targets",
    )(meta, loc, query, *mine, *swapped)

    from_core = swap_core(other)
    from_high = swap_high((keep + from_core).astype(bf16))

    prob = pl.pallas_call(
        functools.partial(logit_kernel, idx_scale),
        out_shape=part,
        in_specs=[smem(), vmem(), vmem(), vmem()],
        out_specs=vmem(),
        scratch_shapes=[
            pltpu.VMEM((2, 2, 2, 512, 128), f32),
            pltpu.VMEM((2, 32, TILE), f32),
            pltpu.VMEM((2, 32, TILE), f32),
        ],
        compiler_params=params(12),
        cost_estimate=pl.CostEstimate(flops=5_000_000_000, bytes_accessed=4_000_000, transcendentals=200_000),
        name="logits",
    )(meta, iq_chip, iq_far, sorted_keys)

    grad = pl.pallas_call(
        gradient_kernel,
        out_shape=jax.ShapeDtypeStruct((TILES, 32, TILE), bf16),
        in_specs=[smem()] + [vmem()] * 4,
        out_specs=vmem(),
        scratch_shapes=[pltpu.VMEM((TILES, 32, TILE), f32), pltpu.VMEM((2, 32, TILE), f32)],
        compiler_params=params(8),
        name="gradient",
    )(meta, prob, keep, from_core, from_high)
    grad_other = swap_core(grad)

    shard = jax.ShapeDtypeStruct((64, 32, 128), f32)
    cost = pl.CostEstimate(flops=5_000_000_000, bytes_accessed=4_000_000, transcendentals=0)
    dk_keep, dk_other = pl.pallas_call(
        functools.partial(key_kernel, idx_scale),
        out_shape=(shard, shard),
        in_specs=[smem(), smem()] + [vmem()] * 5,
        out_specs=(vmem(), vmem()),
        scratch_shapes=[pltpu.VMEM((2, 1024, 128), f32)],
        compiler_params=params(12),
        cost_estimate=cost,
        name="keys",
    )(meta, stored, grad, grad_other, iqw, iqt, sorted_keys)
    dq = pl.pallas_call(
        functools.partial(query_kernel, idx_scale),
        out_shape=jax.ShapeDtypeStruct((2, 1024, 128), f32),
        in_specs=[smem()] + [vmem()] * 4,
        out_specs=vmem(),
        scratch_shapes=[pltpu.VMEM((2, 1024, 128), f32)],
        compiler_params=params(12),
        cost_estimate=cost,
        name="queries",
    )(meta, grad, grad_other, iqw, sorted_keys)

    dk = dk_keep + swap_core(dk_other)
    dk = ring_sum(dk.reshape(4, 4, 4, 32, 128), functools.partial(along, True))
    dk, dq = lax.optimization_barrier((dk, dq))
    dk = ring_sum(dk, functools.partial(along, False))
    dk = ring_sum(dk, lambda shift: lambda x, z, y, k: (x, z + shift, y, k))
    query_grad = dq.reshape(2, 16, HALF, 128).transpose(0, 2, 1, 3).reshape(128, 16, 128)
    return query_grad, dk


def solution(mesh):
    return jax.shard_map(
        per_device,
        mesh=mesh,
        in_specs=(
            P(),
            P("ctx", "head", None),
            P("ctx", None),
            P("ctx", "head"),
            P("ctx", "head", None),
            P("ctx", None),
            P("ctx", "head"),
        ),
        out_specs=(P("ctx", "head", None), P(("ctx", "head"), None)),
        check_vma=False,
    )
```

```python
import functools
import math

import jax
import jax.numpy as jnp
from jax import lax
from jax.experimental import pallas as pl
from jax.experimental.pallas import tpu as pltpu
from jax.sharding import PartitionSpec as P

ALL = ("ctx", "head")
HALF = 64
TILE = 256
PER_TILE = TILE // HALF
TILES = 17
NEAR = 18 * 4
FAR = 8 * 4
SLOT, GOAL, ROW, ROW_OTHER, POSITION, COUNT = 0, 128, 256, 320, 384, 448
MLA_SCALE = 192.0**-0.5
LOSS_SCALE = 64.0
NT = (((1,), (1,)), ((), ()))
NN = (((1,), (0,)), ((), ()))


def permutation(move):
    pairs = []
    for x in range(4):
        for zl in range(2):
            for y in range(4):
                for zh in range(2):
                    for k in range(2):
                        tx, tz, ty, tk = move(x, 2 * zh + zl, y, k)
                        tx, tz, ty, tk = tx % 4, tz % 4, ty % 4, tk % 2
                        source = (x * 8 + zl * 4 + y) * 4 + zh * 2 + k
                        target = (tx * 8 + (tz % 2) * 4 + ty) * 4 + (tz // 2) * 2 + tk
                        pairs.append((source, target))
    return pairs


def send(value, move):
    return lax.ppermute(value, ALL, permutation(move))


def swap_core(value):
    return send(value, lambda x, z, y, k: (x, z, y, k + 1))


def swap_high(value):
    return send(value, lambda x, z, y, k: (x, z + 2, y, k))


def along(first, shift):
    def move(x, z, y, k):
        if (k == 0) == first:
            return (x, z, y + shift, k)
        return (x + shift, z, y, k)

    return move


def vmem():
    return pl.BlockSpec(memory_space=pltpu.VMEM)


def smem():
    return pl.BlockSpec(memory_space=pltpu.SMEM)


def anywhere():
    return pl.BlockSpec(memory_space=pl.ANY)


def params(mib):
    return pltpu.CompilerParams(vmem_limit_bytes=mib * 1024 * 1024)


def place(meta, step):
    half = (step >= meta[0]).astype(jnp.int32)
    return half, step - half * meta[0]


def plan_kernel(meta, order, slot, row, row_other, plan):
    ends = (jnp.int32(0), jnp.int32(NEAR))
    for half in range(2):
        limit = meta[2 + half]

        def step(i, ends, half=half, limit=limit):
            near, far = ends
            position, at = order[i], slot[i]
            if half == 0:
                plan[ROW + position] = row[i]
                plan[ROW_OTHER + position] = row_other[i]
                plan[POSITION + at] = position
            is_far = jnp.where((at // 8) % 4 == 3, 1, 0)
            seen = jnp.where(position <= limit, 1, 0)
            to = jnp.where(seen == 1, jnp.where(is_far == 1, far, near), NEAR + FAR)
            plan[SLOT + to] = at
            plan[GOAL + to] = position + half * PER_TILE * meta[0]
            return near + seen * (1 - is_far), far + seen * is_far

        ends = lax.fori_loop(0, 64, step, ends, unroll=4)
        for part, end in enumerate(ends):
            for u in range(3):
                plan[SLOT + end + u] = 24 * part
                plan[GOAL + end + u] = 68
        ends = ((ends[0] + 3) // 4 * 4, (ends[1] + 3) // 4 * 4)
        plan[COUNT + 2 * half] = ends[0] // 4
        plan[COUNT + 2 * half + 1] = (ends[1] - NEAR) // 4


def pack_kernel(q_ref, n_ref, packed, token, out, sems):
    token[...] = jnp.zeros(token.shape, jnp.int32)
    n = n_ref[...] * -math.sqrt(192.0)
    n1 = n.astype(jnp.bfloat16).astype(jnp.float32)
    n2 = (n - n1).astype(jnp.bfloat16).astype(jnp.float32)
    n3 = n - n1 - n2
    row = lax.broadcasted_iota(jnp.int32, (64, 128), 0)
    copies = []
    for i in range(16):
        lanes = slice(i * 128, (i + 1) * 128)
        a, b = q_ref[2 * i], q_ref[2 * i + 1]
        out[0, 0:576, lanes] = jnp.concatenate((a[:, 0:64], b[:, 0:64]), axis=1)
        out[1, 0:576, lanes] = jnp.concatenate((a[:, 64:128], b[:, 64:128]), axis=1)
        for half in range(2):
            cut = slice(half * 64, half * 64 + 64)
            parts = [
                jnp.concatenate((v[2 * i : 2 * i + 1, cut], v[2 * i + 1 : 2 * i + 2, cut]), axis=1)
                for v in (n1, n2, n3)
            ]
            block = jnp.where(row == 0, parts[0], jnp.where(row == 1, parts[1], jnp.where(row == 2, parts[2], 0.0)))
            out[half, 576:640, lanes] = block.astype(jnp.bfloat16)
        if i % 4 == 3:
            at = pl.ds((i - 3) * 128, 512)
            copies.append(pltpu.make_async_copy(out.at[:, :, at], packed.at[:, :, at], sems.at[i // 4]))
            copies[-1].start()
    for copy in copies:
        copy.wait()


def target_kernel(part, unread, meta, plan, q_ref, *refs):
    count = 3 - part
    groups, refs = (refs[0:count], refs[count : 2 * count]), refs[2 * count :]
    if part == 0:
        sums, sorted_ref, token, keys, sems = refs[unread:]
        token[...] = jnp.zeros(token.shape, jnp.int32)
    else:
        sums, sorted_ref, keep, other, keys, sems = refs[2 + unread :]
    core = meta[1]
    size = 4 if part else 8
    copies = []
    for side, group in enumerate(groups):
        owner = core if side == 0 else 1 - core
        for j, ref in enumerate(group):
            at = owner * 32 + 24 * part + j * size
            copies.append(pltpu.make_async_copy(ref, keys.at[pl.ds(at, size)], sems.at[side * count + j]))
    for copy in copies:
        copy.start()
    for copy in copies:
        copy.wait()
    for owner in range(2):

        def sort(i, _, owner=owner):
            slot = owner * 32 + i
            at = pl.multiple_of(plan[POSITION + slot] * HALF, HALF)
            sorted_ref[pl.ds(at, HALF), :] = keys[slot, :, 640:768]
            return 0

        lax.fori_loop(24 * part, 24 + 8 * part, sort, 0, unroll=4)
    scale = MLA_SCALE * math.log2(math.e)
    first, tiles = plan[COUNT + part], plan[COUNT + 2 + part]

    def body(t):
        half = jnp.where(t >= first, 1, 0)
        at = part * NEAR + t * PER_TILE
        tile = jnp.concatenate([keys[plan[SLOT + at + u], :, 0:640] for u in range(PER_TILE)], axis=0)
        total = jnp.zeros((TILE, 128), jnp.float32)
        for g in range(8):
            s = lax.dot_general(
                tile, q_ref[half, :, g * 256 : (g + 1) * 256], NN, preferred_element_type=jnp.float32
            )
            e = jnp.exp2(s * scale)
            total = total + (e[:, 0:128] + e[:, 128:256])
        for u in range(PER_TILE):
            sums[plan[GOAL + at + u]] = total[u * HALF : (u + 1) * HALF]

    def pair(i, _):
        body(2 * i)
        body(2 * i + 1)
        return 0

    lax.fori_loop(0, tiles // 2, pair, 0)

    @pl.when(tiles % 2 == 1)
    def _():
        body(tiles - 1)

    if part == 1:

        def fold(step, _):
            total = sums[pl.ds(step * PER_TILE, PER_TILE)].reshape(TILE, 128).T
            total = total[0:64] + total[64:128]
            top, low = total[0:32], total[32:64]
            keep[step] = jnp.where(core == 0, top, low)
            other[step] = jnp.where(core == 0, low, top)
            return 0

        lax.fori_loop(0, TILES, fold, 0, unroll=4)


def visible_of(meta, half, ktile):
    rows = lax.broadcasted_iota(jnp.int32, (32, TILE), 0) + meta[1] * 32 + meta[2 + half] * HALF
    cols = lax.broadcasted_iota(jnp.int32, (32, TILE), 1) + ktile * TILE
    return cols <= rows


def logit_kernel(idx_scale, meta, a_ref, b_ref, key_ref, out, wide, top, norm):
    for side, ref in enumerate((a_ref, b_ref)):
        for c in range(2):
            for half in range(2):
                w = ref[c, half, 16].astype(jnp.float32)
                for j in range(16):
                    wide[side, c, half, pl.ds(j * 32, 32)] = jnp.broadcast_to(w[:, j : j + 1], (32, 128))
    top[...] = jnp.full(top.shape, -jnp.inf, jnp.float32)
    norm[...] = jnp.zeros(norm.shape, jnp.float32)

    def first(step, _):
        half, ktile = place(meta, step)
        tile = key_ref[pl.ds(pl.multiple_of(ktile * TILE, TILE), TILE), :]
        total = jnp.zeros((32, TILE), jnp.float32)
        for side, ref in enumerate((a_ref, b_ref)):
            for c in range(2):
                rows = ref[c, half, 0:16].reshape(512, 128)
                d = jnp.maximum(lax.dot_general(rows, tile, NT, preferred_element_type=jnp.float32), 0.0)
                w = wide[side, c, half]
                d = d * jnp.concatenate((w, w), axis=1)
                for j in range(16):
                    total = total + d[j * 32 : (j + 1) * 32]
        logits = jnp.where(visible_of(meta, half, ktile), total * idx_scale, -jnp.inf)
        out[step] = logits
        top[half] = jnp.maximum(top[half], logits)
        return 0

    lax.fori_loop(0, TILES, first, 0, unroll=4)
    for half in range(2):
        top[half] = jnp.broadcast_to(jnp.max(top[half], axis=1, keepdims=True), (32, TILE))

    def second(step, _):
        half, _ktile = place(meta, step)
        e = jnp.exp(out[step] - top[half])
        out[step] = e
        norm[half] = norm[half] + e
        return 0

    lax.fori_loop(0, TILES, second, 0)
    for half in range(2):
        norm[half] = jnp.broadcast_to(1.0 / jnp.sum(norm[half], axis=1, keepdims=True), (32, TILE))

    def third(step, _):
        half, _ktile = place(meta, step)
        out[step] = out[step] * norm[half]
        return 0

    lax.fori_loop(0, TILES, third, 0)


def gradient_kernel(meta, p_ref, a_ref, b_ref, c_ref, out, whole, total):
    total[...] = jnp.zeros(total.shape, jnp.float32)

    def first(step, _):
        half, ktile = place(meta, step)
        t = a_ref[step] + b_ref[step] + c_ref[step].astype(jnp.float32)
        t = jnp.where(visible_of(meta, half, ktile), t, 0.0)
        whole[step] = t
        total[half] = total[half] + t
        return 0

    lax.fori_loop(0, TILES, first, 0)
    for half in range(2):
        total[half] = jnp.broadcast_to(1.0 / jnp.sum(total[half], axis=1, keepdims=True), (32, TILE))

    def second(step, _):
        half, _ktile = place(meta, step)
        out[step] = (LOSS_SCALE * (p_ref[step] - whole[step] * total[half])).astype(jnp.bfloat16)
        return 0

    lax.fori_loop(0, TILES, second, 0)


def spread(iq_ref, wide, idx_scale):
    for half in range(2):
        w = iq_ref[half, 16].astype(jnp.float32) * idx_scale
        for j in range(16):
            wide[half, pl.ds(j * HALF, HALF)] = jnp.broadcast_to(w[:, j : j + 1], (HALF, 128))


def coefficients(meta, step, g_ref, h_ref, iq_ref, key_ref, wide):
    core = meta[1]
    half, ktile = place(meta, step)
    tile = key_ref[pl.ds(pl.multiple_of(ktile * TILE, TILE), TILE), :]
    mine, theirs = g_ref[step].astype(jnp.float32), h_ref[step].astype(jnp.float32)
    g = jnp.concatenate((jnp.where(core == 0, mine, theirs), jnp.where(core == 0, theirs, mine)), axis=0)
    g = jnp.concatenate((g, g, g, g), axis=0)
    found = []
    for q in range(4):
        rows = iq_ref[half, pl.ds(q * 4, 4)].reshape(256, 128)
        d = lax.dot_general(rows, tile, NT, preferred_element_type=jnp.float32)
        w = wide[half, pl.ds(q * 256, 256)]
        found.append(jnp.where(d > 0, g * jnp.concatenate((w, w), axis=1), 0.0).astype(jnp.bfloat16))
    return half, ktile, tile, found


def key_kernel(idx_scale, meta, plan, g_ref, h_ref, iq_ref, iqt_ref, key_ref, keep, other, wide):
    core = meta[1]
    spread(iq_ref, wide, idx_scale)
    keep[...] = jnp.zeros(keep.shape, jnp.float32)
    other[...] = jnp.zeros(other.shape, jnp.float32)

    def body(step, _):
        half, ktile, _tile, found = coefficients(meta, step, g_ref, h_ref, iq_ref, key_ref, wide)
        dkt = lax.dot_general(
            iqt_ref[half], jnp.concatenate(found, axis=0), NN, preferred_element_type=jnp.float32
        )
        dk = dkt.T
        for u in range(PER_TILE):
            slot, slot_other = plan[ROW + ktile * PER_TILE + u], plan[ROW_OTHER + ktile * PER_TILE + u]
            first, last = dk[u * 64 : u * 64 + 32], dk[u * 64 + 32 : u * 64 + 64]
            keep[slot] = keep[slot] + jnp.where(core == 0, first, last)
            other[slot_other] = other[slot_other] + jnp.where(core == 0, last, first)
        return 0

    lax.fori_loop(0, TILES, body, 0, unroll=4)


def query_kernel(idx_scale, meta, g_ref, h_ref, iq_ref, key_ref, dq, token, wide):
    token[...] = jnp.zeros(token.shape, jnp.int32)
    spread(iq_ref, wide, idx_scale)
    dq[...] = jnp.zeros(dq.shape, jnp.float32)

    def body(step, _):
        half, _ktile, tile, found = coefficients(meta, step, g_ref, h_ref, iq_ref, key_ref, wide)
        for q in range(4):
            dq[half, pl.ds(q * 256, 256)] = dq[half, pl.ds(q * 256, 256)] + lax.dot_general(
                found[q], tile, NN, preferred_element_type=jnp.float32
            )
        return 0

    lax.fori_loop(0, TILES, body, 0, unroll=4)


def ring_sum(value, route):
    got = [send(value[shift], route(shift)) for shift in (1, 3, 2)]
    return value[0] + got[0] + got[1] + got[2]


def per_device(
    block_order, query_latent, key_latent, normalizer, indexer_query, indexer_key, indexer_weight
):
    f32, bf16 = jnp.float32, jnp.bfloat16
    idx_scale = 8192.0**-0.5
    ctx, head = lax.axis_index("ctx"), lax.axis_index("head")
    x, zl, y = ctx // 8, (ctx // 4) % 2, ctx % 4
    core = head % 2

    small = pl.CostEstimate(flops=1_000_000, bytes_accessed=1_000_000, transcendentals=0)
    flag = jax.ShapeDtypeStruct((8, 128), jnp.int32)

    index = jnp.arange(64, dtype=jnp.int32)
    bc, bk = index // 2, index % 2
    bx, bz, by = bc // 8, (bc // 4) % 2, bc % 4

    def ring_slot(rel):
        return jnp.where(rel == 0, 0, jnp.where(rel == 3, 1, jnp.where(rel == 1, 2, 3)))

    rx, ry = ring_slot((bx - x) % 4), ring_slot((by - y) % 4)
    rz = (bz != zl).astype(jnp.int32)
    slot = bk * 32 + jnp.where(bk == 0, rx * 8 + ry * 2, ry * 8 + rx * 2) + rz
    blocks = lax.dynamic_slice_in_dim(block_order, ctx * 2, 2, 0)
    qx, qy = (bx - x) % 4, (by - y) % 4
    qz = (2 * bk + bz - 2 * (head // 2) - zl) % 4
    row_a, row_b = qy * 16 + qx * 4 + qz, qx * 16 + qy * 4 + qz
    row_a, row_b = jnp.where(core == 0, row_a, row_b), jnp.where(core == 0, row_b, row_a)
    meta = jnp.concatenate(((blocks[0:1] + PER_TILE) // PER_TILE, core[None], blocks)).astype(jnp.int32)
    plan = pl.pallas_call(
        plan_kernel,
        out_shape=jax.ShapeDtypeStruct((512,), jnp.int32),
        in_specs=[smem()] * 5,
        out_specs=smem(),
        cost_estimate=small,
        name="plan",
    )(meta, block_order, slot, row_a, row_b)

    ones = (lax.broadcasted_iota(jnp.int32, (128, 64), 1) < 3).astype(bf16)
    packed = jnp.concatenate((key_latent, ones, indexer_key), axis=1)
    own = lax.dynamic_slice_in_dim(packed, core * HALF, HALF, 0)
    beside = send(own, lambda x, z, y, k: (x, z + 1 - 2 * k, y, k))
    pair = jnp.stack((own, beside))
    legs = [pair] + [send(pair, along(True, shift)) for shift in (1, 3, 2)]
    group = jnp.concatenate(legs, axis=0)
    query, token = pl.pallas_call(
        pack_kernel,
        out_shape=(jax.ShapeDtypeStruct((2, 640, 2048), bf16), flag),
        in_specs=[vmem(), vmem()],
        out_specs=(pl.BlockSpec(memory_space=pltpu.HBM), vmem()),
        scratch_shapes=[pltpu.VMEM((2, 640, 2048), bf16), pltpu.SemaphoreType.DMA((4,))],
        compiler_params=params(8),
        cost_estimate=small,
        name="pack",
    )(query_latent.transpose(1, 2, 0), normalizer.T)

    iq = indexer_query.reshape(2, HALF, 16, 128).transpose(0, 2, 1, 3)
    weight = jnp.pad(indexer_weight.reshape(2, 1, HALF, 16), ((0, 0), (0, 0), (0, 0), (0, 112)))
    iqw = jnp.concatenate((iq, weight), axis=1)
    iqt = iq.transpose(0, 3, 1, 2).reshape(2, 128, 1024)
    iq_high = swap_high(iqw)
    group, iq_flag = lax.optimization_barrier((group, iq_high[0, 0, 0:8]))
    iq_both = jnp.stack((iqw, iq_high))
    iq_keep = lax.dynamic_slice_in_dim(iq_both, core * 32, 32, 3)
    iq_other = swap_core(lax.dynamic_slice_in_dim(iq_both, (1 - core) * 32, 32, 3))

    up, down = send(group, along(False, 1)), send(group, along(False, 3))
    up, token, plan = lax.optimization_barrier((up, token, plan))
    far_a, far_b = send(up[0:4], along(False, 1)), send(down[4:8], along(False, 3))
    near = [group, up, down]
    near = near + [swap_core(v) for v in near]

    part = jax.ShapeDtypeStruct((TILES, 32, TILE), f32)
    def targets(stage, outs, after, *arrays):
        reads = 6 - 2 * stage
        return pl.pallas_call(
            functools.partial(target_kernel, stage, len(after)),
            out_shape=(jax.ShapeDtypeStruct((69, HALF, 128), f32), jax.ShapeDtypeStruct((4096, 128), bf16)) + outs,
            in_specs=[smem(), smem(), vmem()] + [anywhere()] * reads + [vmem()] * (2 * stage) + [anywhere()] * len(after),
            out_specs=(vmem(),) * (2 + len(outs)),
            scratch_shapes=[pltpu.VMEM((64, HALF, 768), bf16), pltpu.SemaphoreType.DMA((reads,))],
            input_output_aliases={3 + reads: 0, 4 + reads: 1} if stage else {},
            compiler_params=params(14),
            cost_estimate=small,
            name="targets_far" if stage else "targets_near",
        )(meta, plan, query, *arrays, *after)

    sums, sorted_keys, token = targets(0, (flag,), (iq_flag, token, iq_other), *near)
    far_a, far_b, token = lax.optimization_barrier((far_a, far_b, token))
    far = (far_a, far_b, swap_core(far_a), swap_core(far_b))
    _, sorted_keys, keep, other = targets(1, (part, part), (token,), *far, sums, sorted_keys)
    from_core = swap_core(other)
    from_high = swap_high((keep + from_core).astype(bf16))

    prob = pl.pallas_call(
        functools.partial(logit_kernel, idx_scale),
        out_shape=part,
        in_specs=[smem(), vmem(), vmem(), vmem()],
        out_specs=vmem(),
        scratch_shapes=[
            pltpu.VMEM((2, 2, 2, 512, 128), f32),
            pltpu.VMEM((2, 32, TILE), f32),
            pltpu.VMEM((2, 32, TILE), f32),
        ],
        compiler_params=params(12),
        cost_estimate=small,
        name="logits",
    )(meta, iq_keep, iq_other, sorted_keys)

    grad = pl.pallas_call(
        gradient_kernel,
        out_shape=jax.ShapeDtypeStruct((TILES, 32, TILE), bf16),
        in_specs=[smem()] + [vmem()] * 4,
        out_specs=vmem(),
        scratch_shapes=[pltpu.VMEM((TILES, 32, TILE), f32), pltpu.VMEM((2, 32, TILE), f32)],
        compiler_params=params(8),
        cost_estimate=small,
        name="gradient",
    )(meta, prob, keep, from_core, from_high)
    grad_other = swap_core(grad)

    shard = jax.ShapeDtypeStruct((64, 32, 128), f32)
    dk_keep, dk_other = pl.pallas_call(
        functools.partial(key_kernel, idx_scale),
        out_shape=(shard, shard),
        in_specs=[smem(), smem()] + [vmem()] * 5,
        out_specs=(vmem(), vmem()),
        scratch_shapes=[pltpu.VMEM((2, 1024, 128), f32)],
        compiler_params=params(12),
        cost_estimate=small,
        name="keys",
    )(meta, plan, grad, grad_other, iqw, iqt, sorted_keys)
    dq, token = pl.pallas_call(
        functools.partial(query_kernel, idx_scale),
        out_shape=(jax.ShapeDtypeStruct((2, 1024, 128), f32), flag),
        in_specs=[smem()] + [vmem()] * 4,
        out_specs=(vmem(), vmem()),
        scratch_shapes=[pltpu.VMEM((2, 1024, 128), f32)],
        compiler_params=params(12),
        cost_estimate=small,
        name="queries",
    )(meta, grad, grad_other, iqw, sorted_keys)

    dk = dk_keep + swap_core(dk_other)
    dk = ring_sum(dk.reshape(4, 4, 4, 32, 128), functools.partial(along, True))
    dk, token = lax.optimization_barrier((dk, token))
    dk = ring_sum(dk, functools.partial(along, False))
    dk = ring_sum(dk, lambda shift: lambda x, z, y, k: (x, z + shift, y, k))
    query_grad = dq.reshape(2, 16, HALF, 128).transpose(0, 2, 1, 3).reshape(128, 16, 128)
    return query_grad, dk + token[0:1].astype(f32)


def solution(mesh):
    return jax.shard_map(
        per_device,
        mesh=mesh,
        in_specs=(
            P(),
            P("ctx", "head", None),
            P("ctx", None),
            P("ctx", "head"),
            P("ctx", "head", None),
            P("ctx", None),
            P("ctx", "head"),
        ),
        out_specs=(P("ctx", "head", None), P(("ctx", "head"), None)),
        check_vma=False,
    )
```

```python
import functools
import math

import jax
import jax.numpy as jnp
from jax import lax
from jax.experimental import pallas as pl
from jax.experimental.pallas import tpu as pltpu
from jax.sharding import PartitionSpec as P

ALL = ("ctx", "head")
HALF = 64
TILE = 256
PER_TILE = TILE // HALF
TILES = 17
NEAR = 18 * 4
FAR = 8 * 4
SLOT, GOAL, ROW, ROW_OTHER, POSITION, COUNT = 0, 128, 256, 320, 384, 448
MLA_SCALE = 192.0**-0.5
LOSS_SCALE = 64.0
NT = (((1,), (1,)), ((), ()))
NN = (((1,), (0,)), ((), ()))


def permutation(move):
    pairs = []
    for x in range(4):
        for zl in range(2):
            for y in range(4):
                for zh in range(2):
                    for k in range(2):
                        tx, tz, ty, tk = move(x, 2 * zh + zl, y, k)
                        tx, tz, ty, tk = tx % 4, tz % 4, ty % 4, tk % 2
                        source = (x * 8 + zl * 4 + y) * 4 + zh * 2 + k
                        target = (tx * 8 + (tz % 2) * 4 + ty) * 4 + (tz // 2) * 2 + tk
                        pairs.append((source, target))
    return pairs


def send(value, move):
    return lax.ppermute(value, ALL, permutation(move))


def swap_core(value):
    return send(value, lambda x, z, y, k: (x, z, y, k + 1))


def swap_high(value):
    return send(value, lambda x, z, y, k: (x, z + 2, y, k))


def along(first, shift):
    def move(x, z, y, k):
        if (k == 0) == first:
            return (x, z, y + shift, k)
        return (x + shift, z, y, k)

    return move


def vmem():
    return pl.BlockSpec(memory_space=pltpu.VMEM)


def smem():
    return pl.BlockSpec(memory_space=pltpu.SMEM)


def anywhere():
    return pl.BlockSpec(memory_space=pl.ANY)


def params(mib):
    return pltpu.CompilerParams(vmem_limit_bytes=mib * 1024 * 1024)


def place(meta, step):
    half = (step >= meta[0]).astype(jnp.int32)
    return half, step - half * meta[0]


def plan_kernel(meta, order, slot, row, row_other, plan):
    ends = (jnp.int32(0), jnp.int32(NEAR))
    for half in range(2):
        limit = meta[2 + half]

        def step(i, ends, half=half, limit=limit):
            near, far = ends
            position, at = order[i], slot[i]
            if half == 0:
                plan[ROW + position] = row[i]
                plan[ROW_OTHER + position] = row_other[i]
                plan[POSITION + at] = position
            is_far = jnp.where((at // 8) % 4 == 3, 1, 0)
            seen = jnp.where(position <= limit, 1, 0)
            to = jnp.where(seen == 1, jnp.where(is_far == 1, far, near), NEAR + FAR)
            plan[SLOT + to] = at
            plan[GOAL + to] = position + half * PER_TILE * meta[0]
            return near + seen * (1 - is_far), far + seen * is_far

        ends = lax.fori_loop(0, 64, step, ends, unroll=4)
        for part, end in enumerate(ends):
            for u in range(3):
                plan[SLOT + end + u] = 24 * part
                plan[GOAL + end + u] = 68
        ends = ((ends[0] + 3) // 4 * 4, (ends[1] + 3) // 4 * 4)
        plan[COUNT + 2 * half] = ends[0] // 4
        plan[COUNT + 2 * half + 1] = (ends[1] - NEAR) // 4


def pack(q_ref, n_ref, out):
    n = n_ref[...] * -math.sqrt(192.0)
    n1 = n.astype(jnp.bfloat16).astype(jnp.float32)
    n2 = (n - n1).astype(jnp.bfloat16).astype(jnp.float32)
    n3 = n - n1 - n2
    row = lax.broadcasted_iota(jnp.int32, (64, 128), 0)
    for i in range(16):
        lanes = slice(i * 128, (i + 1) * 128)
        a, b = q_ref[2 * i], q_ref[2 * i + 1]
        out[0, 0:576, lanes] = jnp.concatenate((a[:, 0:64], b[:, 0:64]), axis=1)
        out[1, 0:576, lanes] = jnp.concatenate((a[:, 64:128], b[:, 64:128]), axis=1)
        for half in range(2):
            cut = slice(half * 64, half * 64 + 64)
            parts = [
                jnp.concatenate((v[2 * i : 2 * i + 1, cut], v[2 * i + 1 : 2 * i + 2, cut]), axis=1)
                for v in (n1, n2, n3)
            ]
            block = jnp.where(row == 0, parts[0], jnp.where(row == 1, parts[1], jnp.where(row == 2, parts[2], 0.0)))
            out[half, 576:640, lanes] = block.astype(jnp.bfloat16)


def target_kernel(part, unread, meta, plan, q_ref, *refs):
    count = 3 - part
    groups, refs = (refs[0:count], refs[count : 2 * count]), refs[2 * count :]
    if part == 0:
        n_ref, (sums, sorted_ref, token, packed, keys, sems) = refs[0], refs[1 + unread :]
        token[...] = jnp.zeros(token.shape, jnp.int32)
    else:
        sums, sorted_ref, keep, other, keys, sems = refs[2 + unread :]
    core = meta[1]
    size = 4 if part else 8
    copies = []
    for side, group in enumerate(groups):
        owner = core if side == 0 else 1 - core
        for j, ref in enumerate(group):
            at = owner * 32 + 24 * part + j * size
            copies.append(pltpu.make_async_copy(ref, keys.at[pl.ds(at, size)], sems.at[side * count + j]))
    for copy in copies:
        copy.start()
    if part == 0:
        pack(q_ref, n_ref, packed)
        q_ref = packed
    for copy in copies:
        copy.wait()
    for owner in range(2):

        def sort(i, _, owner=owner):
            slot = owner * 32 + i
            at = pl.multiple_of(plan[POSITION + slot] * HALF, HALF)
            sorted_ref[pl.ds(at, HALF), :] = keys[slot, :, 640:768]
            return 0

        lax.fori_loop(24 * part, 24 + 8 * part, sort, 0, unroll=4)
    scale = MLA_SCALE * math.log2(math.e)
    first, tiles = plan[COUNT + part], plan[COUNT + 2 + part]

    def body(t):
        half = jnp.where(t >= first, 1, 0)
        at = part * NEAR + t * PER_TILE
        tile = jnp.concatenate([keys[plan[SLOT + at + u], :, 0:640] for u in range(PER_TILE)], axis=0)
        total = jnp.zeros((TILE, 128), jnp.float32)
        for g in range(8):
            s = lax.dot_general(
                tile, q_ref[half, :, g * 256 : (g + 1) * 256], NN, preferred_element_type=jnp.float32
            )
            e = jnp.exp2(s * scale)
            total = total + (e[:, 0:128] + e[:, 128:256])
        for u in range(PER_TILE):
            sums[plan[GOAL + at + u]] = total[u * HALF : (u + 1) * HALF]

    def pair(i, _):
        body(2 * i)
        body(2 * i + 1)
        return 0

    lax.fori_loop(0, tiles // 2, pair, 0)

    @pl.when(tiles % 2 == 1)
    def _():
        body(tiles - 1)

    if part == 1:

        def fold(step, _):
            total = sums[pl.ds(step * PER_TILE, PER_TILE)].reshape(TILE, 128).T
            total = total[0:64] + total[64:128]
            top, low = total[0:32], total[32:64]
            keep[step] = jnp.where(core == 0, top, low)
            other[step] = jnp.where(core == 0, low, top)
            return 0

        lax.fori_loop(0, TILES, fold, 0, unroll=4)


def visible_of(meta, half, ktile):
    rows = lax.broadcasted_iota(jnp.int32, (32, TILE), 0) + meta[1] * 32 + meta[2 + half] * HALF
    cols = lax.broadcasted_iota(jnp.int32, (32, TILE), 1) + ktile * TILE
    return cols <= rows


def logit_kernel(idx_scale, meta, a_ref, b_ref, key_ref, out, wide, top, norm):
    for side, ref in enumerate((a_ref, b_ref)):
        for c in range(2):
            for half in range(2):
                w = ref[c, half, 16].astype(jnp.float32)
                for j in range(16):
                    wide[side, c, half, pl.ds(j * 32, 32)] = jnp.broadcast_to(w[:, j : j + 1], (32, 128))
    top[...] = jnp.full(top.shape, -jnp.inf, jnp.float32)
    norm[...] = jnp.zeros(norm.shape, jnp.float32)

    def first(step, _):
        half, ktile = place(meta, step)
        tile = key_ref[pl.ds(pl.multiple_of(ktile * TILE, TILE), TILE), :]
        total = jnp.zeros((32, TILE), jnp.float32)
        for side, ref in enumerate((a_ref, b_ref)):
            for c in range(2):
                rows = ref[c, half, 0:16].reshape(512, 128)
                d = jnp.maximum(lax.dot_general(rows, tile, NT, preferred_element_type=jnp.float32), 0.0)
                w = wide[side, c, half]
                d = d * jnp.concatenate((w, w), axis=1)
                for j in range(16):
                    total = total + d[j * 32 : (j + 1) * 32]
        logits = jnp.where(visible_of(meta, half, ktile), total * idx_scale, -jnp.inf)
        out[step] = logits
        top[half] = jnp.maximum(top[half], logits)
        return 0

    lax.fori_loop(0, TILES, first, 0, unroll=4)
    for half in range(2):
        top[half] = jnp.broadcast_to(jnp.max(top[half], axis=1, keepdims=True), (32, TILE))

    def second(step, _):
        half, _ktile = place(meta, step)
        e = jnp.exp(out[step] - top[half])
        out[step] = e
        norm[half] = norm[half] + e
        return 0

    lax.fori_loop(0, TILES, second, 0)
    for half in range(2):
        norm[half] = jnp.broadcast_to(1.0 / jnp.sum(norm[half], axis=1, keepdims=True), (32, TILE))

    def third(step, _):
        half, _ktile = place(meta, step)
        out[step] = out[step] * norm[half]
        return 0

    lax.fori_loop(0, TILES, third, 0)


def gradient_kernel(meta, p_ref, a_ref, b_ref, c_ref, out, whole, total):
    total[...] = jnp.zeros(total.shape, jnp.float32)

    def first(step, _):
        half, ktile = place(meta, step)
        t = a_ref[step] + b_ref[step] + c_ref[step].astype(jnp.float32)
        t = jnp.where(visible_of(meta, half, ktile), t, 0.0)
        whole[step] = t
        total[half] = total[half] + t
        return 0

    lax.fori_loop(0, TILES, first, 0)
    for half in range(2):
        total[half] = jnp.broadcast_to(1.0 / jnp.sum(total[half], axis=1, keepdims=True), (32, TILE))

    def second(step, _):
        half, _ktile = place(meta, step)
        out[step] = (LOSS_SCALE * (p_ref[step] - whole[step] * total[half])).astype(jnp.bfloat16)
        return 0

    lax.fori_loop(0, TILES, second, 0)


def spread(iq_ref, wide, idx_scale):
    for half in range(2):
        w = iq_ref[half, 16].astype(jnp.float32) * idx_scale
        for j in range(16):
            wide[half, pl.ds(j * HALF, HALF)] = jnp.broadcast_to(w[:, j : j + 1], (HALF, 128))


def coefficients(meta, step, g_ref, h_ref, iq_ref, key_ref, wide, groups=(0, 1, 2, 3)):
    core = meta[1]
    half, ktile = place(meta, step)
    tile = key_ref[pl.ds(pl.multiple_of(ktile * TILE, TILE), TILE), :]
    mine, theirs = g_ref[step].astype(jnp.float32), h_ref[step].astype(jnp.float32)
    g = jnp.concatenate((jnp.where(core == 0, mine, theirs), jnp.where(core == 0, theirs, mine)), axis=0)
    g = jnp.concatenate((g, g, g, g), axis=0)
    found = []
    for q in groups:
        rows = iq_ref[half, pl.ds(q * 4, 4)].reshape(256, 128)
        d = lax.dot_general(rows, tile, NT, preferred_element_type=jnp.float32)
        w = wide[half, pl.ds(q * 256, 256)]
        found.append(jnp.where(d > 0, g * jnp.concatenate((w, w), axis=1), 0.0).astype(jnp.bfloat16))
    return half, ktile, tile, found


def key_kernel(idx_scale, meta, plan, g_ref, h_ref, iq_ref, iqt_ref, key_ref, keep, other, wide):
    core = meta[1]
    spread(iq_ref, wide, idx_scale)
    keep[...] = jnp.zeros(keep.shape, jnp.float32)
    other[...] = jnp.zeros(other.shape, jnp.float32)

    def body(step, _):
        half, ktile, _tile, found = coefficients(meta, step, g_ref, h_ref, iq_ref, key_ref, wide)
        dkt = lax.dot_general(
            iqt_ref[half], jnp.concatenate(found, axis=0), NN, preferred_element_type=jnp.float32
        )
        dk = dkt.T
        for u in range(PER_TILE):
            slot, slot_other = plan[ROW + ktile * PER_TILE + u], plan[ROW_OTHER + ktile * PER_TILE + u]
            first, last = dk[u * 64 : u * 64 + 32], dk[u * 64 + 32 : u * 64 + 64]
            keep[slot] = keep[slot] + jnp.where(core == 0, first, last)
            other[slot_other] = other[slot_other] + jnp.where(core == 0, last, first)
        return 0

    lax.fori_loop(0, TILES, body, 0, unroll=4)


def query_kernel(groups, idx_scale, meta, g_ref, h_ref, iq_ref, key_ref, *refs):
    dq, token, wide = refs[-3:]
    token[...] = jnp.zeros(token.shape, jnp.int32)
    spread(iq_ref, wide, idx_scale)
    dq[...] = jnp.zeros(dq.shape, jnp.float32)

    def body(step, _):
        half, _ktile, tile, found = coefficients(meta, step, g_ref, h_ref, iq_ref, key_ref, wide, groups)
        for q in range(2):
            dq[half, pl.ds(q * 256, 256)] = dq[half, pl.ds(q * 256, 256)] + lax.dot_general(
                found[q], tile, NN, preferred_element_type=jnp.float32
            )
        return 0

    lax.fori_loop(0, TILES, body, 0, unroll=4)


def ring_sum(value, route):
    got = [send(value[shift], route(shift)) for shift in (1, 3, 2)]
    return value[0] + got[0] + got[1] + got[2]


def per_device(
    block_order, query_latent, key_latent, normalizer, indexer_query, indexer_key, indexer_weight
):
    f32, bf16 = jnp.float32, jnp.bfloat16
    idx_scale = 8192.0**-0.5
    ctx, head = lax.axis_index("ctx"), lax.axis_index("head")
    x, zl, y = ctx // 8, (ctx // 4) % 2, ctx % 4
    core = head % 2

    small = pl.CostEstimate(flops=1_000_000, bytes_accessed=1_000_000, transcendentals=0)
    flag = jax.ShapeDtypeStruct((8, 128), jnp.int32)

    index = jnp.arange(64, dtype=jnp.int32)
    bc, bk = index // 2, index % 2
    bx, bz, by = bc // 8, (bc // 4) % 2, bc % 4

    def ring_slot(rel):
        return jnp.where(rel == 0, 0, jnp.where(rel == 3, 1, jnp.where(rel == 1, 2, 3)))

    rx, ry = ring_slot((bx - x) % 4), ring_slot((by - y) % 4)
    rz = (bz != zl).astype(jnp.int32)
    slot = bk * 32 + jnp.where(bk == 0, rx * 8 + ry * 2, ry * 8 + rx * 2) + rz
    blocks = lax.dynamic_slice_in_dim(block_order, ctx * 2, 2, 0)
    qx, qy = (bx - x) % 4, (by - y) % 4
    qz = (2 * bk + bz - 2 * (head // 2) - zl) % 4
    row_a, row_b = qy * 16 + qx * 4 + qz, qx * 16 + qy * 4 + qz
    row_a, row_b = jnp.where(core == 0, row_a, row_b), jnp.where(core == 0, row_b, row_a)
    meta = jnp.concatenate(((blocks[0:1] + PER_TILE) // PER_TILE, core[None], blocks)).astype(jnp.int32)
    plan = pl.pallas_call(
        plan_kernel,
        out_shape=jax.ShapeDtypeStruct((512,), jnp.int32),
        in_specs=[smem()] * 5,
        out_specs=smem(),
        cost_estimate=small,
        name="plan",
    )(meta, block_order, slot, row_a, row_b)

    ones = (lax.broadcasted_iota(jnp.int32, (128, 64), 1) < 3).astype(bf16)
    packed = jnp.concatenate((key_latent, ones, indexer_key), axis=1)
    own = lax.dynamic_slice_in_dim(packed, core * HALF, HALF, 0)
    beside = send(own, lambda x, z, y, k: (x, z + 1 - 2 * k, y, k))
    pair = jnp.stack((own, beside))
    legs = [pair] + [send(pair, along(True, shift)) for shift in (1, 3, 2)]
    group = jnp.concatenate(legs, axis=0)
    iq = indexer_query.reshape(2, HALF, 16, 128).transpose(0, 2, 1, 3)
    weight = jnp.pad(indexer_weight.reshape(2, 1, HALF, 16), ((0, 0), (0, 0), (0, 0), (0, 112)))
    iqw = jnp.concatenate((iq, weight), axis=1)
    iqt = iq.transpose(0, 3, 1, 2).reshape(2, 128, 1024)
    iq_high = swap_high(iqw)
    group, iq_flag = lax.optimization_barrier((group, iq_high[0, 0, 0:8]))
    iq_both = jnp.stack((iqw, iq_high))
    iq_keep = lax.dynamic_slice_in_dim(iq_both, core * 32, 32, 3)
    iq_other = swap_core(lax.dynamic_slice_in_dim(iq_both, (1 - core) * 32, 32, 3))

    up, down = send(group, along(False, 1)), send(group, along(False, 3))
    up, plan = lax.optimization_barrier((up, plan))
    far_a, far_b = send(up[0:4], along(False, 1)), send(down[4:8], along(False, 3))
    near = [group, up, down]
    near = near + [swap_core(v) for v in near]

    part = jax.ShapeDtypeStruct((TILES, 32, TILE), f32)
    def targets(stage, outs, after, *arrays):
        reads = 6 - 2 * stage
        held = len(arrays) - 1 - reads
        return pl.pallas_call(
            functools.partial(target_kernel, stage, len(after)),
            out_shape=(jax.ShapeDtypeStruct((69, HALF, 128), f32), jax.ShapeDtypeStruct((4096, 128), bf16)) + outs,
            in_specs=[smem(), smem(), vmem()] + [anywhere()] * reads + [vmem()] * held + [anywhere()] * len(after),
            out_specs=(vmem(),) * (2 + len(outs)),
            scratch_shapes=[pltpu.VMEM((64, HALF, 768), bf16), pltpu.SemaphoreType.DMA((reads,))],
            input_output_aliases={3 + reads: 0, 4 + reads: 1} if stage else {},
            compiler_params=params(20),
            cost_estimate=small,
            name="targets_far" if stage else "targets_near",
        )(meta, plan, *arrays, *after)

    sums, sorted_keys, token, query = targets(
        0,
        (flag, jax.ShapeDtypeStruct((2, 640, 2048), bf16)),
        (iq_flag, iq_other),
        query_latent.transpose(1, 2, 0),
        *near,
        normalizer.T,
    )
    far_a, far_b, token = lax.optimization_barrier((far_a, far_b, token))
    far = (far_a, far_b, swap_core(far_a), swap_core(far_b))
    _, sorted_keys, keep, other = targets(
        1, (part, part), (token,), query, *far, sums, sorted_keys
    )
    from_core = swap_core(other)
    from_high = swap_high((keep + from_core).astype(bf16))

    prob = pl.pallas_call(
        functools.partial(logit_kernel, idx_scale),
        out_shape=part,
        in_specs=[smem(), vmem(), vmem(), vmem()],
        out_specs=vmem(),
        scratch_shapes=[
            pltpu.VMEM((2, 2, 2, 512, 128), f32),
            pltpu.VMEM((2, 32, TILE), f32),
            pltpu.VMEM((2, 32, TILE), f32),
        ],
        compiler_params=params(12),
        cost_estimate=small,
        name="logits",
    )(meta, iq_keep, iq_other, sorted_keys)

    grad = pl.pallas_call(
        gradient_kernel,
        out_shape=jax.ShapeDtypeStruct((TILES, 32, TILE), bf16),
        in_specs=[smem()] + [vmem()] * 4,
        out_specs=vmem(),
        scratch_shapes=[pltpu.VMEM((TILES, 32, TILE), f32), pltpu.VMEM((2, 32, TILE), f32)],
        compiler_params=params(8),
        cost_estimate=small,
        name="gradient",
    )(meta, prob, keep, from_core, from_high)
    grad_other = swap_core(grad)

    shard = jax.ShapeDtypeStruct((64, 32, 128), f32)
    dk_keep, dk_other = pl.pallas_call(
        functools.partial(key_kernel, idx_scale),
        out_shape=(shard, shard),
        in_specs=[smem(), smem()] + [vmem()] * 5,
        out_specs=(vmem(), vmem()),
        scratch_shapes=[pltpu.VMEM((2, 1024, 128), f32)],
        compiler_params=params(12),
        cost_estimate=small,
        name="keys",
    )(meta, plan, grad, grad_other, iqw, iqt, sorted_keys)
    def queries(groups, *after):
        return pl.pallas_call(
            functools.partial(query_kernel, groups, idx_scale),
            out_shape=(jax.ShapeDtypeStruct((2, 512, 128), f32), flag),
            in_specs=[smem()] + [vmem()] * 4 + [anywhere()] * len(after),
            out_specs=(vmem(), vmem()),
            scratch_shapes=[pltpu.VMEM((2, 1024, 128), f32)],
            compiler_params=params(12),
            cost_estimate=small,
            name="queries",
        )(meta, grad, grad_other, iqw, sorted_keys, *after)

    dk = dk_keep + swap_core(dk_other)
    low, token = queries((0, 1))
    dk = ring_sum(dk.reshape(4, 4, 4, 32, 128), functools.partial(along, True))
    dk, token = lax.optimization_barrier((dk, token))
    high, token = queries((2, 3), token)
    dk = ring_sum(dk, functools.partial(along, False))
    dk, token, low, high = lax.optimization_barrier((dk, token, low, high))
    dk = ring_sum(dk, lambda shift: lambda x, z, y, k: (x, z + shift, y, k))
    low, high = [v.reshape(2, 8, HALF, 128).transpose(0, 2, 1, 3).reshape(128, 8, 128) for v in (low, high)]
    query_grad = jnp.concatenate((low, high), axis=1)
    return query_grad, dk + token[0:1].astype(f32)


def solution(mesh):
    return jax.shard_map(
        per_device,
        mesh=mesh,
        in_specs=(
            P(),
            P("ctx", "head", None),
            P("ctx", None),
            P("ctx", "head"),
            P("ctx", "head", None),
            P("ctx", None),
            P("ctx", "head"),
        ),
        out_specs=(P("ctx", "head", None), P(("ctx", "head"), None)),
        check_vma=False,
    )
```

```python
import functools
import math

import jax
import jax.numpy as jnp
from jax import lax
from jax.experimental import pallas as pl
from jax.experimental.pallas import tpu as pltpu
from jax.sharding import PartitionSpec as P

ALL = ("ctx", "head")
HALF = 64
TILE = 256
PER_TILE = TILE // HALF
TILES = 17
LISTS = (0, 8 * 4, 24 * 4)
UNUSED = 32 * 4
SLOT, GOAL, ROW, ROW_OTHER, POSITION, COUNT = 0, 256, 512, 576, 640, 704
MLA_SCALE = 192.0**-0.5
LOSS_SCALE = 64.0
NT = (((1,), (1,)), ((), ()))
NN = (((1,), (0,)), ((), ()))


def permutation(move):
    pairs = []
    for x in range(4):
        for zl in range(2):
            for y in range(4):
                for zh in range(2):
                    for k in range(2):
                        tx, tz, ty, tk = move(x, 2 * zh + zl, y, k)
                        tx, tz, ty, tk = tx % 4, tz % 4, ty % 4, tk % 2
                        source = (x * 8 + zl * 4 + y) * 4 + zh * 2 + k
                        target = (tx * 8 + (tz % 2) * 4 + ty) * 4 + (tz // 2) * 2 + tk
                        pairs.append((source, target))
    return pairs


def send(value, move):
    return lax.ppermute(value, ALL, permutation(move))


def swap_core(value):
    return send(value, lambda x, z, y, k: (x, z, y, k + 1))


def swap_high(value):
    return send(value, lambda x, z, y, k: (x, z + 2, y, k))


def along(first, shift):
    def move(x, z, y, k):
        if (k == 0) == first:
            return (x, z, y + shift, k)
        return (x + shift, z, y, k)

    return move


def vmem():
    return pl.BlockSpec(memory_space=pltpu.VMEM)


def smem():
    return pl.BlockSpec(memory_space=pltpu.SMEM)


def anywhere():
    return pl.BlockSpec(memory_space=pl.ANY)


def params(mib):
    return pltpu.CompilerParams(vmem_limit_bytes=mib * 1024 * 1024)


def place(meta, step):
    half = (step >= meta[0]).astype(jnp.int32)
    return half, step - half * meta[0]


def plan_kernel(meta, order, slot, row, row_other, plan):
    ends = tuple(jnp.int32(start) for start in LISTS)
    for half in range(2):
        limit, base = meta[2 + half], half * PER_TILE * meta[0]

        def step(i, ends, half=half, limit=limit, base=base):
            position, at = order[i], slot[i]
            if half == 0:
                plan[ROW + position] = row[i]
                plan[ROW_OTHER + position] = row_other[i]
                plan[POSITION + at] = position
            ring = (at // 8) % 4
            stage = jnp.where(ring == 0, 0, jnp.where(ring == 3, 2, 1))
            seen = jnp.where(position <= limit, 1, 0)
            to = jnp.where(stage == 0, ends[0], jnp.where(stage == 1, ends[1], ends[2]))
            to = jnp.where(seen == 1, to, UNUSED)
            plan[SLOT + to] = at
            plan[GOAL + to] = position + base
            return tuple(end + jnp.where(stage == part, seen, 0) for part, end in enumerate(ends))

        ends = lax.fori_loop(0, 64, step, ends, unroll=4)
        for part, end in enumerate(ends):
            for u in range(3):
                plan[SLOT + end + u] = (0, 8, 24)[part]
                plan[GOAL + end + u] = 68
        ends = tuple((end + 3) // 4 * 4 for end in ends)
        for part, end in enumerate(ends):
            plan[COUNT + 3 * half + part] = (end - LISTS[part]) // 4


def pack(q_ref, n_ref, out):
    n = n_ref[...] * -math.sqrt(192.0)
    n1 = n.astype(jnp.bfloat16).astype(jnp.float32)
    n2 = (n - n1).astype(jnp.bfloat16).astype(jnp.float32)
    n3 = n - n1 - n2
    row = lax.broadcasted_iota(jnp.int32, (64, 128), 0)
    for i in range(16):
        lanes = slice(i * 128, (i + 1) * 128)
        a, b = q_ref[2 * i], q_ref[2 * i + 1]
        out[0, 0:576, lanes] = jnp.concatenate((a[:, 0:64], b[:, 0:64]), axis=1)
        out[1, 0:576, lanes] = jnp.concatenate((a[:, 64:128], b[:, 64:128]), axis=1)
        for half in range(2):
            cut = slice(half * 64, half * 64 + 64)
            parts = [
                jnp.concatenate((v[2 * i : 2 * i + 1, cut], v[2 * i + 1 : 2 * i + 2, cut]), axis=1)
                for v in (n1, n2, n3)
            ]
            block = jnp.where(row == 0, parts[0], jnp.where(row == 1, parts[1], jnp.where(row == 2, parts[2], 0.0)))
            out[half, 576:640, lanes] = block.astype(jnp.bfloat16)


def target_kernel(stage, unread, meta, plan, q_ref, *refs):
    count, size, base = ((1, 8, 0), (2, 8, 8), (2, 4, 24))[stage]
    groups, refs = (refs[0:count], refs[count : 2 * count]), refs[2 * count :]
    n_ref, keys, sems = refs[0], refs[-2], refs[-1]
    refs = refs[(2 if stage else 1) + unread : -2]
    if stage == 0:
        sums, sorted_ref, token, packed = refs
    elif stage == 1:
        sums, sorted_ref, token = refs
    else:
        sums, sorted_ref, keep, other = refs
    if stage < 2:
        token[...] = jnp.zeros(token.shape, jnp.int32)
    core = meta[1]
    copies = []
    for side, group in enumerate(groups):
        owner = core if side == 0 else 1 - core
        for j, ref in enumerate(group):
            at = owner * 32 + base + j * size
            copies.append(pltpu.make_async_copy(ref, keys.at[pl.ds(at, size)], sems.at[side * count + j]))
    for copy in copies:
        copy.start()
    if stage == 0:
        pack(q_ref, n_ref, packed)
        q_ref = packed
    for copy in copies:
        copy.wait()
    for owner in range(2):

        def sort(i, _, owner=owner):
            slot = owner * 32 + i
            at = pl.multiple_of(plan[POSITION + slot] * HALF, HALF)
            sorted_ref[pl.ds(at, HALF), :] = keys[slot, :, 640:768]
            return 0

        lax.fori_loop(base, base + count * size, sort, 0, unroll=4)
    scale = MLA_SCALE * math.log2(math.e)
    first, tiles = plan[COUNT + stage], plan[COUNT + 3 + stage]

    def body(t):
        half = jnp.where(t >= first, 1, 0)
        at = LISTS[stage] + t * PER_TILE
        tile = jnp.concatenate([keys[plan[SLOT + at + u], :, 0:640] for u in range(PER_TILE)], axis=0)
        total = jnp.zeros((TILE, 128), jnp.float32)
        for g in range(8):
            s = lax.dot_general(
                tile, q_ref[half, :, g * 256 : (g + 1) * 256], NN, preferred_element_type=jnp.float32
            )
            e = jnp.exp2(s * scale)
            total = total + (e[:, 0:128] + e[:, 128:256])
        for u in range(PER_TILE):
            sums[plan[GOAL + at + u]] = total[u * HALF : (u + 1) * HALF]

    def pair(i, _):
        body(2 * i)
        body(2 * i + 1)
        return 0

    lax.fori_loop(0, tiles // 2, pair, 0)

    @pl.when(tiles % 2 == 1)
    def _():
        body(tiles - 1)

    if stage == 2:

        def fold(step, _):
            total = sums[pl.ds(step * PER_TILE, PER_TILE)].reshape(TILE, 128).T
            total = total[0:64] + total[64:128]
            top, low = total[0:32], total[32:64]
            keep[step] = jnp.where(core == 0, top, low)
            other[step] = jnp.where(core == 0, low, top)
            return 0

        lax.fori_loop(0, TILES, fold, 0, unroll=4)


def take_kernel(start, source, out, sem):
    copy = pltpu.make_async_copy(source.at[pl.ds(start, 4)], out, sem)
    copy.start()
    copy.wait()


def visible_of(meta, half, ktile):
    rows = lax.broadcasted_iota(jnp.int32, (32, TILE), 0) + meta[1] * 32 + meta[2 + half] * HALF
    cols = lax.broadcasted_iota(jnp.int32, (32, TILE), 1) + ktile * TILE
    return cols <= rows


def logit_kernel(idx_scale, meta, a_ref, b_ref, key_ref, iq_ref, out, scaled, wide, top, norm):
    spread(iq_ref, scaled, idx_scale)
    for side, ref in enumerate((a_ref, b_ref)):
        for c in range(2):
            for half in range(2):
                w = ref[c, half, 16].astype(jnp.float32)
                for j in range(16):
                    wide[side, c, half, pl.ds(j * 32, 32)] = jnp.broadcast_to(w[:, j : j + 1], (32, 128))
    top[...] = jnp.full(top.shape, -jnp.inf, jnp.float32)
    norm[...] = jnp.zeros(norm.shape, jnp.float32)

    def first(step, _):
        half, ktile = place(meta, step)
        tile = key_ref[pl.ds(pl.multiple_of(ktile * TILE, TILE), TILE), :]
        total = jnp.zeros((32, TILE), jnp.float32)
        for side, ref in enumerate((a_ref, b_ref)):
            for c in range(2):
                rows = ref[c, half, 0:16].reshape(512, 128)
                d = jnp.maximum(lax.dot_general(rows, tile, NT, preferred_element_type=jnp.float32), 0.0)
                w = wide[side, c, half]
                d = d * jnp.concatenate((w, w), axis=1)
                for j in range(16):
                    total = total + d[j * 32 : (j + 1) * 32]
        logits = jnp.where(visible_of(meta, half, ktile), total * idx_scale, -jnp.inf)
        out[step] = logits
        top[half] = jnp.maximum(top[half], logits)
        return 0

    lax.fori_loop(0, TILES, first, 0, unroll=4)
    for half in range(2):
        top[half] = jnp.broadcast_to(jnp.max(top[half], axis=1, keepdims=True), (32, TILE))

    def second(step, _):
        half, _ktile = place(meta, step)
        e = jnp.exp(out[step] - top[half])
        out[step] = e
        norm[half] = norm[half] + e
        return 0

    lax.fori_loop(0, TILES, second, 0)
    for half in range(2):
        norm[half] = jnp.broadcast_to(1.0 / jnp.sum(norm[half], axis=1, keepdims=True), (32, TILE))

    def third(step, _):
        half, _ktile = place(meta, step)
        out[step] = out[step] * norm[half]
        return 0

    lax.fori_loop(0, TILES, third, 0)


def gradient_kernel(meta, p_ref, a_ref, b_ref, c_ref, out, whole, total):
    total[...] = jnp.zeros(total.shape, jnp.float32)

    def first(step, _):
        half, ktile = place(meta, step)
        t = a_ref[step] + b_ref[step] + c_ref[step].astype(jnp.float32)
        t = jnp.where(visible_of(meta, half, ktile), t, 0.0)
        whole[step] = t
        total[half] = total[half] + t
        return 0

    lax.fori_loop(0, TILES, first, 0)
    for half in range(2):
        total[half] = jnp.broadcast_to(1.0 / jnp.sum(total[half], axis=1, keepdims=True), (32, TILE))

    def second(step, _):
        half, _ktile = place(meta, step)
        out[step] = (LOSS_SCALE * (p_ref[step] - whole[step] * total[half])).astype(jnp.bfloat16)
        return 0

    lax.fori_loop(0, TILES, second, 0)


def spread(iq_ref, wide, idx_scale):
    for half in range(2):
        w = iq_ref[half, 16].astype(jnp.float32) * idx_scale
        for j in range(16):
            wide[half, pl.ds(j * HALF, HALF)] = jnp.broadcast_to(w[:, j : j + 1], (HALF, 128))


def coefficients(meta, step, g_ref, h_ref, iq_ref, key_ref, wide, groups=(0, 1, 2, 3)):
    core = meta[1]
    half, ktile = place(meta, step)
    tile = key_ref[pl.ds(pl.multiple_of(ktile * TILE, TILE), TILE), :]
    mine, theirs = g_ref[step].astype(jnp.float32), h_ref[step].astype(jnp.float32)
    g = jnp.concatenate((jnp.where(core == 0, mine, theirs), jnp.where(core == 0, theirs, mine)), axis=0)
    g = jnp.concatenate((g, g, g, g), axis=0)
    found = []
    for q in groups:
        rows = iq_ref[half, pl.ds(q * 4, 4)].reshape(256, 128)
        d = lax.dot_general(rows, tile, NT, preferred_element_type=jnp.float32)
        w = wide[half, pl.ds(q * 256, 256)]
        found.append(jnp.where(d > 0, g * jnp.concatenate((w, w), axis=1), 0.0).astype(jnp.bfloat16))
    return half, ktile, tile, found


def key_kernel(meta, plan, g_ref, h_ref, iq_ref, iqt_ref, key_ref, wide, keep, other):
    core = meta[1]
    keep[...] = jnp.zeros(keep.shape, jnp.float32)
    other[...] = jnp.zeros(other.shape, jnp.float32)

    def body(step, _):
        half, ktile, _tile, found = coefficients(meta, step, g_ref, h_ref, iq_ref, key_ref, wide)
        dkt = lax.dot_general(
            iqt_ref[half], jnp.concatenate(found, axis=0), NN, preferred_element_type=jnp.float32
        )
        dk = dkt.T
        for u in range(PER_TILE):
            slot, slot_other = plan[ROW + ktile * PER_TILE + u], plan[ROW_OTHER + ktile * PER_TILE + u]
            first, last = dk[u * 64 : u * 64 + 32], dk[u * 64 + 32 : u * 64 + 64]
            keep[slot] = keep[slot] + jnp.where(core == 0, first, last)
            other[slot_other] = other[slot_other] + jnp.where(core == 0, last, first)
        return 0

    lax.fori_loop(0, TILES, body, 0, unroll=4)


def query_kernel(groups, meta, g_ref, h_ref, iq_ref, key_ref, wide, *refs):
    dq, token = refs[-2:]
    token[...] = jnp.zeros(token.shape, jnp.int32)
    dq[...] = jnp.zeros(dq.shape, jnp.float32)

    def body(step, _):
        half, _ktile, tile, found = coefficients(meta, step, g_ref, h_ref, iq_ref, key_ref, wide, groups)
        for q in range(2):
            dq[half, pl.ds(q * 256, 256)] = dq[half, pl.ds(q * 256, 256)] + lax.dot_general(
                found[q], tile, NN, preferred_element_type=jnp.float32
            )
        return 0

    lax.fori_loop(0, TILES, body, 0, unroll=4)


def ring_sum(value, route):
    got = [send(value[shift], route(shift)) for shift in (1, 3, 2)]
    return value[0] + got[0] + got[1] + got[2]


def per_device(
    block_order, query_latent, key_latent, normalizer, indexer_query, indexer_key, indexer_weight
):
    f32, bf16 = jnp.float32, jnp.bfloat16
    idx_scale = 8192.0**-0.5
    ctx, head = lax.axis_index("ctx"), lax.axis_index("head")
    x, zl, y = ctx // 8, (ctx // 4) % 2, ctx % 4
    core = head % 2

    small = pl.CostEstimate(flops=1_000_000, bytes_accessed=1_000_000, transcendentals=0)
    flag = jax.ShapeDtypeStruct((8, 128), jnp.int32)
    part = jax.ShapeDtypeStruct((TILES, 32, TILE), f32)

    index = jnp.arange(64, dtype=jnp.int32)
    bc, bk = index // 2, index % 2
    bx, bz, by = bc // 8, (bc // 4) % 2, bc % 4

    def ring_slot(rel):
        return jnp.where(rel == 0, 0, jnp.where(rel == 3, 1, jnp.where(rel == 1, 2, 3)))

    rx, ry = ring_slot((bx - x) % 4), ring_slot((by - y) % 4)
    rz = (bz != zl).astype(jnp.int32)
    slot = bk * 32 + jnp.where(bk == 0, rx * 8 + ry * 2, ry * 8 + rx * 2) + rz
    blocks = lax.dynamic_slice_in_dim(block_order, ctx * 2, 2, 0)
    qx, qy = (bx - x) % 4, (by - y) % 4
    qz = (2 * bk + bz - 2 * (head // 2) - zl) % 4
    row_a, row_b = qy * 16 + qx * 4 + qz, qx * 16 + qy * 4 + qz
    row_a, row_b = jnp.where(core == 0, row_a, row_b), jnp.where(core == 0, row_b, row_a)
    meta = jnp.concatenate(((blocks[0:1] + PER_TILE) // PER_TILE, core[None], blocks)).astype(jnp.int32)
    plan = pl.pallas_call(
        plan_kernel,
        out_shape=jax.ShapeDtypeStruct((768,), jnp.int32),
        in_specs=[smem()] * 5,
        out_specs=smem(),
        compiler_params=params(1),
        cost_estimate=small,
        name="plan",
    )(meta, block_order, slot, row_a, row_b)

    ones = (lax.broadcasted_iota(jnp.int32, (128, 64), 1) < 3).astype(bf16)
    packed = jnp.concatenate((key_latent, ones, indexer_key), axis=1)
    own = lax.dynamic_slice_in_dim(packed, core * HALF, HALF, 0)
    beside = send(own, lambda x, z, y, k: (x, z + 1 - 2 * k, y, k))
    pair = jnp.stack((own, beside))
    legs = [pair] + [send(pair, along(True, shift)) for shift in (1, 3, 2)]
    group = jnp.concatenate(legs, axis=0)
    iq = indexer_query.reshape(2, HALF, 16, 128).transpose(0, 2, 1, 3)
    weight = jnp.pad(indexer_weight.reshape(2, 1, HALF, 16), ((0, 0), (0, 0), (0, 0), (0, 112)))
    iqw = jnp.concatenate((iq, weight), axis=1)
    iqt = iq.transpose(0, 3, 1, 2).reshape(2, 128, 1024)
    iq_high = swap_high(iqw)
    group, plan, iq_flag = lax.optimization_barrier((group, plan, iq_high[0, 0, 0:8]))
    iq_both = jnp.stack((iqw, iq_high))
    iq_keep = lax.dynamic_slice_in_dim(iq_both, core * 32, 32, 3)
    iq_send = lax.dynamic_slice_in_dim(iq_both, (1 - core) * 32, 32, 3)
    iq_other = swap_core(iq_send)

    def targets(stage, outs, after, *arrays):
        reads = (2, 4, 4)[stage]
        held = len(arrays) - 1 - reads
        return pl.pallas_call(
            functools.partial(target_kernel, stage, len(after)),
            out_shape=(jax.ShapeDtypeStruct((69, HALF, 128), f32), jax.ShapeDtypeStruct((4096, 128), bf16)) + outs,
            in_specs=[smem(), smem(), vmem()] + [anywhere()] * reads + [vmem()] * held + [anywhere()] * len(after),
            out_specs=(vmem(),) * (2 + len(outs)),
            scratch_shapes=[pltpu.VMEM((64, HALF, 768), bf16), pltpu.SemaphoreType.DMA((reads,))],
            input_output_aliases={3 + reads: 0, 4 + reads: 1} if stage else {},
            compiler_params=params(16),
            cost_estimate=small,
            name=("targets_first", "targets_near", "targets_far")[stage],
        )(meta, plan, *arrays, *after)

    def take(value, start, after):
        return pl.pallas_call(
            lambda source, _after, out, sem: take_kernel(start, source, out, sem),
            out_shape=jax.ShapeDtypeStruct((4, HALF, 768), bf16),
            in_specs=[anywhere(), anywhere()],
            out_specs=anywhere(),
            scratch_shapes=[pltpu.SemaphoreType.DMA],
            compiler_params=params(1),
            cost_estimate=small,
            name="take",
        )(value, after)

    up, down = send(group, along(False, 1)), send(group, along(False, 3))
    sums, sorted_keys, token, query = targets(
        0,
        (flag, jax.ShapeDtypeStruct((2, 640, 2048), bf16)),
        (iq_keep, iq_send),
        query_latent.transpose(1, 2, 0),
        group,
        swap_core(group),
        normalizer.T,
    )
    up, down, token = lax.optimization_barrier((up, down, token))
    far_a = send(take(up, 0, token), along(False, 1))
    far_b = send(take(down, 4, token), along(False, 3))
    near = (up, down, swap_core(up), swap_core(down))
    sums, sorted_keys, token = targets(1, (flag,), (token, iq_flag, iq_other), query, *near, sums, sorted_keys)
    far_a, far_b, token = lax.optimization_barrier((far_a, far_b, token))
    far = (far_a, far_b, swap_core(far_a), swap_core(far_b))
    _, sorted_keys, keep, other = targets(2, (part, part), (token,), query, *far, sums, sorted_keys)
    from_core = swap_core(other)
    from_high = swap_high((keep + from_core).astype(bf16))

    prob, scaled = pl.pallas_call(
        functools.partial(logit_kernel, idx_scale),
        out_shape=(part, jax.ShapeDtypeStruct((2, 1024, 128), f32)),
        in_specs=[smem()] + [vmem()] * 4,
        out_specs=(vmem(), vmem()),
        scratch_shapes=[
            pltpu.VMEM((2, 2, 2, 512, 128), f32),
            pltpu.VMEM((2, 32, TILE), f32),
            pltpu.VMEM((2, 32, TILE), f32),
        ],
        compiler_params=params(12),
        cost_estimate=small,
        name="logits",
    )(meta, iq_keep, iq_other, sorted_keys, iqw)

    grad = pl.pallas_call(
        gradient_kernel,
        out_shape=jax.ShapeDtypeStruct((TILES, 32, TILE), bf16),
        in_specs=[smem()] + [vmem()] * 4,
        out_specs=vmem(),
        scratch_shapes=[pltpu.VMEM((TILES, 32, TILE), f32), pltpu.VMEM((2, 32, TILE), f32)],
        compiler_params=params(8),
        cost_estimate=small,
        name="gradient",
    )(meta, prob, keep, from_core, from_high)
    grad_other = swap_core(grad)

    shard = jax.ShapeDtypeStruct((64, 32, 128), f32)
    dk_keep, dk_other = pl.pallas_call(
        key_kernel,
        out_shape=(shard, shard),
        in_specs=[smem(), smem()] + [vmem()] * 6,
        out_specs=(vmem(), vmem()),
        compiler_params=params(12),
        cost_estimate=small,
        name="keys",
    )(meta, plan, grad, grad_other, iqw, iqt, sorted_keys, scaled)
    def queries(groups, *after):
        return pl.pallas_call(
            functools.partial(query_kernel, groups),
            out_shape=(jax.ShapeDtypeStruct((2, 512, 128), f32), flag),
            in_specs=[smem()] + [vmem()] * 5 + [anywhere()] * len(after),
            out_specs=(vmem(), vmem()),
            compiler_params=params(12),
            cost_estimate=small,
            name="queries",
        )(meta, grad, grad_other, iqw, sorted_keys, scaled, *after)

    dk = dk_keep + swap_core(dk_other)
    low, token = queries((0, 1))
    dk = ring_sum(dk.reshape(4, 4, 4, 32, 128), functools.partial(along, True))
    dk, token = lax.optimization_barrier((dk, token))
    high, token = queries((2, 3), token)
    dk = ring_sum(dk, functools.partial(along, False))
    dk, token, low, high = lax.optimization_barrier((dk, token, low, high))
    dk = ring_sum(dk, lambda shift: lambda x, z, y, k: (x, z + shift, y, k))
    low, high = [v.reshape(2, 8, HALF, 128).transpose(0, 2, 1, 3).reshape(128, 8, 128) for v in (low, high)]
    query_grad = jnp.concatenate((low, high), axis=1)
    return query_grad, dk + token[0:1].astype(f32)


def solution(mesh):
    return jax.shard_map(
        per_device,
        mesh=mesh,
        in_specs=(
            P(),
            P("ctx", "head", None),
            P("ctx", None),
            P("ctx", "head"),
            P("ctx", "head", None),
            P("ctx", None),
            P("ctx", "head"),
        ),
        out_specs=(P("ctx", "head", None), P(("ctx", "head"), None)),
        check_vma=False,
    )
```

```python
import functools
import math

import jax
import jax.numpy as jnp
from jax import lax
from jax.experimental import pallas as pl
from jax.experimental.pallas import tpu as pltpu
from jax.sharding import PartitionSpec as P

ALL = ("ctx", "head")
HALF = 64
TILE = 256
PER_TILE = TILE // HALF
TILES = 17
LISTS = ((0, 16), (32, 64), (96, 112))
UNUSED = 32 * 4
SLOT, GOAL, ROW, ROW_OTHER, POSITION, COUNT = 0, 256, 512, 576, 640, 704
MLA_SCALE = 192.0**-0.5
LOSS_SCALE = 64.0
NT = (((1,), (1,)), ((), ()))
NN = (((1,), (0,)), ((), ()))


def permutation(move):
    pairs = []
    for x in range(4):
        for zl in range(2):
            for y in range(4):
                for zh in range(2):
                    for k in range(2):
                        tx, tz, ty, tk = move(x, 2 * zh + zl, y, k)
                        tx, tz, ty, tk = tx % 4, tz % 4, ty % 4, tk % 2
                        source = (x * 8 + zl * 4 + y) * 4 + zh * 2 + k
                        target = (tx * 8 + (tz % 2) * 4 + ty) * 4 + (tz // 2) * 2 + tk
                        pairs.append((source, target))
    return pairs


def send(value, move):
    return lax.ppermute(value, ALL, permutation(move))


def swap_core(value):
    return send(value, lambda x, z, y, k: (x, z, y, k + 1))


def swap_high(value):
    return send(value, lambda x, z, y, k: (x, z + 2, y, k))


def along(first, shift):
    def move(x, z, y, k):
        if (k == 0) == first:
            return (x, z, y + shift, k)
        return (x + shift, z, y, k)

    return move


def vmem():
    return pl.BlockSpec(memory_space=pltpu.VMEM)


def smem():
    return pl.BlockSpec(memory_space=pltpu.SMEM)


def anywhere():
    return pl.BlockSpec(memory_space=pl.ANY)


def params(mib):
    return pltpu.CompilerParams(vmem_limit_bytes=mib * 1024 * 1024)


def place(meta, step):
    half = (step >= meta[0]).astype(jnp.int32)
    return half, step - half * meta[0]


def plan_kernel(meta, order, slot, row, row_other, _after, plan):
    base = PER_TILE * meta[0]

    def step(i, ends):
        position, at = order[i], slot[i]
        plan[ROW + position] = row[i]
        plan[ROW_OTHER + position] = row_other[i]
        plan[POSITION + at] = position
        ring = (at // 8) % 4
        stage = jnp.where(ring == 0, 0, jnp.where(ring == 3, 2, 1))
        later = []
        for half in range(2):
            mine = ends[3 * half : 3 * half + 3]
            seen = jnp.where(position <= meta[2 + half], 1, 0)
            to = jnp.where(stage == 0, mine[0], jnp.where(stage == 1, mine[1], mine[2]))
            to = jnp.where(seen == 1, to, UNUSED)
            plan[SLOT + to] = at
            plan[GOAL + to] = position + base * half
            later += [end + jnp.where(stage == part, seen, 0) for part, end in enumerate(mine)]
        return tuple(later)

    ends = tuple(jnp.int32(LISTS[part][half]) for half in range(2) for part in range(3))
    ends = lax.fori_loop(0, 64, step, ends, unroll=8)
    for half in range(2):
        for part in range(3):
            end = ends[3 * half + part]
            tiles = (end - LISTS[part][half] + 3) // 4
            plan[COUNT + 3 * half + part] = tiles
            for u in range(3):
                to = jnp.where(end + u < LISTS[part][half] + 4 * tiles, end + u, UNUSED)
                plan[SLOT + to] = (0, 8, 24)[part]
                plan[GOAL + to] = 68


def pack(q_ref, n_ref, out):
    n = n_ref[...] * -math.sqrt(192.0)
    n1 = n.astype(jnp.bfloat16).astype(jnp.float32)
    n2 = (n - n1).astype(jnp.bfloat16).astype(jnp.float32)
    n3 = n - n1 - n2
    row = lax.broadcasted_iota(jnp.int32, (64, 128), 0)
    for i in range(16):
        lanes = slice(i * 128, (i + 1) * 128)
        a, b = q_ref[2 * i], q_ref[2 * i + 1]
        out[0, 0:576, lanes] = jnp.concatenate((a[:, 0:64], b[:, 0:64]), axis=1)
        out[1, 0:576, lanes] = jnp.concatenate((a[:, 64:128], b[:, 64:128]), axis=1)
        for half in range(2):
            cut = slice(half * 64, half * 64 + 64)
            parts = [
                jnp.concatenate((v[2 * i : 2 * i + 1, cut], v[2 * i + 1 : 2 * i + 2, cut]), axis=1)
                for v in (n1, n2, n3)
            ]
            block = jnp.where(row == 0, parts[0], jnp.where(row == 1, parts[1], jnp.where(row == 2, parts[2], 0.0)))
            out[half, 576:640, lanes] = block.astype(jnp.bfloat16)


def target_kernel(stage, unread, meta, plan, q_ref, *refs):
    count, size, base = ((1, 8, 0), (2, 8, 8), (2, 4, 24))[stage]
    groups, refs = (refs[0:count], refs[count : 2 * count]), refs[2 * count :]
    n_ref, keys, sems = refs[0], refs[-2], refs[-1]
    refs = refs[(2 if stage else 1) + unread : -2]
    if stage == 0:
        sums, sorted_ref, token, packed = refs
    elif stage == 1:
        sums, sorted_ref, token = refs
    else:
        sums, sorted_ref, keep, other = refs
    if stage < 2:
        token[...] = jnp.zeros(token.shape, jnp.int32)
    core = meta[1]
    copies = []
    for side, group in enumerate(groups):
        owner = core if side == 0 else 1 - core
        for j, ref in enumerate(group):
            at = owner * 32 + base + j * size
            copies.append(pltpu.make_async_copy(ref, keys.at[pl.ds(at, size)], sems.at[side * count + j]))
    for copy in copies:
        copy.start()
    if stage == 0:
        pack(q_ref, n_ref, packed)
        q_ref = packed
    for copy in copies:
        copy.wait()
    for owner in range(2):

        def sort(i, _, owner=owner):
            slot = owner * 32 + i
            at = pl.multiple_of(plan[POSITION + slot] * HALF, HALF)
            sorted_ref[pl.ds(at, HALF), :] = keys[slot, :, 640:768]
            return 0

        lax.fori_loop(base, base + count * size, sort, 0, unroll=4)
    scale = MLA_SCALE * math.log2(math.e)
    first = plan[COUNT + stage]
    tiles = first + plan[COUNT + 3 + stage]

    def body(t):
        half = jnp.where(t >= first, 1, 0)
        at = LISTS[stage][0] + t * PER_TILE + half * (LISTS[stage][1] - LISTS[stage][0] - first * PER_TILE)
        tile = jnp.concatenate([keys[plan[SLOT + at + u], :, 0:640] for u in range(PER_TILE)], axis=0)
        total = jnp.zeros((TILE, 128), jnp.float32)
        for g in range(8):
            s = lax.dot_general(
                tile, q_ref[half, :, g * 256 : (g + 1) * 256], NN, preferred_element_type=jnp.float32
            )
            e = jnp.exp2(s * scale)
            total = total + (e[:, 0:128] + e[:, 128:256])
        for u in range(PER_TILE):
            sums[plan[GOAL + at + u]] = total[u * HALF : (u + 1) * HALF]

    def pair(i, _):
        body(2 * i)
        body(2 * i + 1)
        return 0

    lax.fori_loop(0, tiles // 2, pair, 0)

    @pl.when(tiles % 2 == 1)
    def _():
        body(tiles - 1)

    if stage == 2:

        def fold(step, _):
            total = sums[pl.ds(step * PER_TILE, PER_TILE)].reshape(TILE, 128).T
            total = total[0:64] + total[64:128]
            top, low = total[0:32], total[32:64]
            keep[step] = jnp.where(core == 0, top, low)
            other[step] = jnp.where(core == 0, low, top)
            return 0

        lax.fori_loop(0, TILES, fold, 0, unroll=4)


def take_kernel(start, source, out, sem):
    copy = pltpu.make_async_copy(source.at[pl.ds(start, 4)], out, sem)
    copy.start()
    copy.wait()


def visible_of(meta, half, ktile):
    rows = lax.broadcasted_iota(jnp.int32, (32, TILE), 0) + meta[1] * 32 + meta[2 + half] * HALF
    cols = lax.broadcasted_iota(jnp.int32, (32, TILE), 1) + ktile * TILE
    return cols <= rows


def logit_kernel(idx_scale, meta, a_ref, b_ref, key_ref, iq_ref, out, scaled, iqt, wide, top, norm):
    for half in range(2):
        iqt[half] = iq_ref[half, 0:16].reshape(1024, 128).T
    spread(iq_ref, scaled, idx_scale)
    for side, ref in enumerate((a_ref, b_ref)):
        for c in range(2):
            for half in range(2):
                w = ref[c, half, 16].astype(jnp.float32)
                for j in range(16):
                    wide[side, c, half, pl.ds(j * 32, 32)] = jnp.broadcast_to(w[:, j : j + 1], (32, 128))
    top[...] = jnp.full(top.shape, -jnp.inf, jnp.float32)
    norm[...] = jnp.zeros(norm.shape, jnp.float32)

    def first(step, _):
        half, ktile = place(meta, step)
        tile = key_ref[pl.ds(pl.multiple_of(ktile * TILE, TILE), TILE), :]
        total = jnp.zeros((32, TILE), jnp.float32)
        for side, ref in enumerate((a_ref, b_ref)):
            for c in range(2):
                rows = ref[c, half, 0:16].reshape(512, 128)
                d = jnp.maximum(lax.dot_general(rows, tile, NT, preferred_element_type=jnp.float32), 0.0)
                w = wide[side, c, half]
                d = d * jnp.concatenate((w, w), axis=1)
                for j in range(16):
                    total = total + d[j * 32 : (j + 1) * 32]
        logits = jnp.where(visible_of(meta, half, ktile), total * idx_scale, -jnp.inf)
        out[step] = logits
        top[half] = jnp.maximum(top[half], logits)
        return 0

    lax.fori_loop(0, TILES, first, 0, unroll=4)
    for half in range(2):
        top[half] = jnp.broadcast_to(jnp.max(top[half], axis=1, keepdims=True), (32, TILE))

    def second(step, _):
        half, _ktile = place(meta, step)
        e = jnp.exp(out[step] - top[half])
        out[step] = e
        norm[half] = norm[half] + e
        return 0

    lax.fori_loop(0, TILES, second, 0)
    for half in range(2):
        norm[half] = jnp.broadcast_to(1.0 / jnp.sum(norm[half], axis=1, keepdims=True), (32, TILE))

    def third(step, _):
        half, _ktile = place(meta, step)
        out[step] = out[step] * norm[half]
        return 0

    lax.fori_loop(0, TILES, third, 0)


def gradient_kernel(meta, p_ref, a_ref, b_ref, c_ref, out, whole, total):
    total[...] = jnp.zeros(total.shape, jnp.float32)

    def first(step, _):
        half, ktile = place(meta, step)
        t = a_ref[step] + b_ref[step] + c_ref[step].astype(jnp.float32)
        t = jnp.where(visible_of(meta, half, ktile), t, 0.0)
        whole[step] = t
        total[half] = total[half] + t
        return 0

    lax.fori_loop(0, TILES, first, 0)
    for half in range(2):
        total[half] = jnp.broadcast_to(1.0 / jnp.sum(total[half], axis=1, keepdims=True), (32, TILE))

    def second(step, _):
        half, _ktile = place(meta, step)
        out[step] = (LOSS_SCALE * (p_ref[step] - whole[step] * total[half])).astype(jnp.bfloat16)
        return 0

    lax.fori_loop(0, TILES, second, 0)


def spread(iq_ref, wide, idx_scale):
    for half in range(2):
        w = iq_ref[half, 16].astype(jnp.float32) * idx_scale
        for j in range(16):
            wide[half, pl.ds(j * HALF, HALF)] = jnp.broadcast_to(w[:, j : j + 1], (HALF, 128))


def coefficients(meta, step, g_ref, h_ref, iq_ref, key_ref, wide, groups=(0, 1, 2, 3)):
    core = meta[1]
    half, ktile = place(meta, step)
    tile = key_ref[pl.ds(pl.multiple_of(ktile * TILE, TILE), TILE), :]
    mine, theirs = g_ref[step].astype(jnp.float32), h_ref[step].astype(jnp.float32)
    g = jnp.concatenate((jnp.where(core == 0, mine, theirs), jnp.where(core == 0, theirs, mine)), axis=0)
    g = jnp.concatenate((g, g, g, g), axis=0)
    found = []
    for q in groups:
        rows = iq_ref[half, pl.ds(q * 4, 4)].reshape(256, 128)
        d = lax.dot_general(rows, tile, NT, preferred_element_type=jnp.float32)
        w = wide[half, pl.ds(q * 256, 256)]
        found.append(jnp.where(d > 0, g * jnp.concatenate((w, w), axis=1), 0.0).astype(jnp.bfloat16))
    return half, ktile, tile, found


def key_kernel(meta, plan, g_ref, h_ref, iq_ref, iqt_ref, key_ref, wide, keep, other):
    core = meta[1]
    keep[...] = jnp.zeros(keep.shape, jnp.float32)
    other[...] = jnp.zeros(other.shape, jnp.float32)

    def body(step, _):
        half, ktile, _tile, found = coefficients(meta, step, g_ref, h_ref, iq_ref, key_ref, wide)
        dkt = lax.dot_general(
            iqt_ref[half], jnp.concatenate(found, axis=0), NN, preferred_element_type=jnp.float32
        )
        dk = dkt.T
        for u in range(PER_TILE):
            slot, slot_other = plan[ROW + ktile * PER_TILE + u], plan[ROW_OTHER + ktile * PER_TILE + u]
            first, last = dk[u * 64 : u * 64 + 32], dk[u * 64 + 32 : u * 64 + 64]
            keep[slot] = keep[slot] + jnp.where(core == 0, first, last)
            other[slot_other] = other[slot_other] + jnp.where(core == 0, last, first)
        return 0

    lax.fori_loop(0, TILES, body, 0, unroll=4)


def query_kernel(groups, meta, g_ref, h_ref, iq_ref, key_ref, wide, *refs):
    dq, token = refs[-2:]
    token[...] = jnp.zeros(token.shape, jnp.int32)
    dq[...] = jnp.zeros(dq.shape, jnp.float32)

    def body(step, _):
        half, _ktile, tile, found = coefficients(meta, step, g_ref, h_ref, iq_ref, key_ref, wide, groups)
        for q in range(2):
            dq[half, pl.ds(q * 256, 256)] = dq[half, pl.ds(q * 256, 256)] + lax.dot_general(
                found[q], tile, NN, preferred_element_type=jnp.float32
            )
        return 0

    lax.fori_loop(0, TILES, body, 0, unroll=4)


def ring_sum(value, route):
    got = [send(value[shift], route(shift)) for shift in (1, 3, 2)]
    return value[0] + got[0] + got[1] + got[2]


def per_device(
    block_order, query_latent, key_latent, normalizer, indexer_query, indexer_key, indexer_weight
):
    f32, bf16 = jnp.float32, jnp.bfloat16
    idx_scale = 8192.0**-0.5
    ctx, head = lax.axis_index("ctx"), lax.axis_index("head")
    x, zl, y = ctx // 8, (ctx // 4) % 2, ctx % 4
    core = head % 2

    small = pl.CostEstimate(flops=1_000_000, bytes_accessed=1_000_000, transcendentals=0)
    flag = jax.ShapeDtypeStruct((8, 128), jnp.int32)
    part = jax.ShapeDtypeStruct((TILES, 32, TILE), f32)

    index = jnp.arange(64, dtype=jnp.int32)
    bc, bk = index // 2, index % 2
    bx, bz, by = bc // 8, (bc // 4) % 2, bc % 4

    def ring_slot(rel):
        return jnp.where(rel == 0, 0, jnp.where(rel == 3, 1, jnp.where(rel == 1, 2, 3)))

    rx, ry = ring_slot((bx - x) % 4), ring_slot((by - y) % 4)
    rz = (bz != zl).astype(jnp.int32)
    slot = bk * 32 + jnp.where(bk == 0, rx * 8 + ry * 2, ry * 8 + rx * 2) + rz
    blocks = lax.dynamic_slice_in_dim(block_order, ctx * 2, 2, 0)
    qx, qy = (bx - x) % 4, (by - y) % 4
    qz = (2 * bk + bz - 2 * (head // 2) - zl) % 4
    row_a, row_b = qy * 16 + qx * 4 + qz, qx * 16 + qy * 4 + qz
    row_a, row_b = jnp.where(core == 0, row_a, row_b), jnp.where(core == 0, row_b, row_a)
    meta = jnp.concatenate(((blocks[0:1] + PER_TILE) // PER_TILE, core[None], blocks)).astype(jnp.int32)
    ones = (lax.broadcasted_iota(jnp.int32, (128, 64), 1) < 3).astype(bf16)
    packed = jnp.concatenate((key_latent, ones, indexer_key), axis=1)
    own = lax.dynamic_slice_in_dim(packed, core * HALF, HALF, 0)
    beside = send(own, lambda x, z, y, k: (x, z + 1 - 2 * k, y, k))
    pair = jnp.stack((own, beside))
    plan = pl.pallas_call(
        plan_kernel,
        out_shape=jax.ShapeDtypeStruct((768,), jnp.int32),
        in_specs=[smem()] * 5 + [anywhere()],
        out_specs=smem(),
        compiler_params=params(1),
        cost_estimate=small,
        name="plan",
    )(meta, block_order, slot, row_a, row_b, pair)
    legs = [pair] + [send(pair, along(True, shift)) for shift in (1, 3, 2)]
    group = jnp.concatenate(legs, axis=0)
    iq = indexer_query.reshape(2, HALF, 16, 128).transpose(0, 2, 1, 3)
    weight = jnp.pad(indexer_weight.reshape(2, 1, HALF, 16), ((0, 0), (0, 0), (0, 0), (0, 112)))
    iqw = jnp.concatenate((iq, weight), axis=1)
    iq_high = swap_high(iqw)
    group, plan, iq_flag = lax.optimization_barrier((group, plan, iq_high[0, 0, 0:8]))
    iq_both = jnp.stack((iqw, iq_high))
    iq_keep = lax.dynamic_slice_in_dim(iq_both, core * 32, 32, 3)
    iq_send = lax.dynamic_slice_in_dim(iq_both, (1 - core) * 32, 32, 3)
    iq_other = swap_core(iq_send)

    def targets(stage, outs, after, *arrays):
        reads = (2, 4, 4)[stage]
        held = len(arrays) - 1 - reads
        return pl.pallas_call(
            functools.partial(target_kernel, stage, len(after)),
            out_shape=(jax.ShapeDtypeStruct((69, HALF, 128), f32), jax.ShapeDtypeStruct((4096, 128), bf16)) + outs,
            in_specs=[smem(), smem(), vmem()] + [anywhere()] * reads + [vmem()] * held + [anywhere()] * len(after),
            out_specs=(vmem(),) * (2 + len(outs)),
            scratch_shapes=[pltpu.VMEM((64, HALF, 768), bf16), pltpu.SemaphoreType.DMA((reads,))],
            input_output_aliases={3 + reads: 0, 4 + reads: 1} if stage else {},
            compiler_params=params(16),
            cost_estimate=small,
            name=("targets_first", "targets_near", "targets_far")[stage],
        )(meta, plan, *arrays, *after)

    def take(value, start, after):
        return pl.pallas_call(
            lambda source, _after, out, sem: take_kernel(start, source, out, sem),
            out_shape=jax.ShapeDtypeStruct((4, HALF, 768), bf16),
            in_specs=[anywhere(), anywhere()],
            out_specs=anywhere(),
            scratch_shapes=[pltpu.SemaphoreType.DMA],
            compiler_params=params(1),
            cost_estimate=small,
            name="take",
        )(value, after)

    up, down = send(group, along(False, 1)), send(group, along(False, 3))
    sums, sorted_keys, token, query = targets(
        0,
        (flag, jax.ShapeDtypeStruct((2, 640, 2048), bf16)),
        (iq_keep, iq_send),
        query_latent.transpose(1, 2, 0),
        group,
        swap_core(group),
        normalizer.T,
    )
    up, down, token = lax.optimization_barrier((up, down, token))
    far_a = send(take(up, 0, token), along(False, 1))
    far_b = send(take(down, 4, token), along(False, 3))
    near = (up, down, swap_core(up), swap_core(down))
    sums, sorted_keys, token = targets(1, (flag,), (token, iq_flag, iq_other), query, *near, sums, sorted_keys)
    far_a, far_b, token = lax.optimization_barrier((far_a, far_b, token))
    far = (far_a, far_b, swap_core(far_a), swap_core(far_b))
    _, sorted_keys, keep, other = targets(2, (part, part), (token,), query, *far, sums, sorted_keys)
    from_core = swap_core(other)
    from_high = swap_high((keep + from_core).astype(bf16))

    prob, scaled, iqt = pl.pallas_call(
        functools.partial(logit_kernel, idx_scale),
        out_shape=(part, jax.ShapeDtypeStruct((2, 1024, 128), f32), jax.ShapeDtypeStruct((2, 128, 1024), bf16)),
        in_specs=[smem()] + [vmem()] * 4,
        out_specs=(vmem(), vmem(), vmem()),
        scratch_shapes=[
            pltpu.VMEM((2, 2, 2, 512, 128), f32),
            pltpu.VMEM((2, 32, TILE), f32),
            pltpu.VMEM((2, 32, TILE), f32),
        ],
        compiler_params=params(12),
        cost_estimate=small,
        name="logits",
    )(meta, iq_keep, iq_other, sorted_keys, iqw)

    grad = pl.pallas_call(
        gradient_kernel,
        out_shape=jax.ShapeDtypeStruct((TILES, 32, TILE), bf16),
        in_specs=[smem()] + [vmem()] * 4,
        out_specs=vmem(),
        scratch_shapes=[pltpu.VMEM((TILES, 32, TILE), f32), pltpu.VMEM((2, 32, TILE), f32)],
        compiler_params=params(8),
        cost_estimate=small,
        name="gradient",
    )(meta, prob, keep, from_core, from_high)
    grad_other = swap_core(grad)

    shard = jax.ShapeDtypeStruct((64, 32, 128), f32)
    dk_keep, dk_other = pl.pallas_call(
        key_kernel,
        out_shape=(shard, shard),
        in_specs=[smem(), smem()] + [vmem()] * 6,
        out_specs=(vmem(), vmem()),
        compiler_params=params(12),
        cost_estimate=small,
        name="keys",
    )(meta, plan, grad, grad_other, iqw, iqt, sorted_keys, scaled)
    def queries(groups, *after):
        return pl.pallas_call(
            functools.partial(query_kernel, groups),
            out_shape=(jax.ShapeDtypeStruct((2, 512, 128), f32), flag),
            in_specs=[smem()] + [vmem()] * 5 + [anywhere()] * len(after),
            out_specs=(vmem(), vmem()),
            compiler_params=params(12),
            cost_estimate=small,
            name="queries",
        )(meta, grad, grad_other, iqw, sorted_keys, scaled, *after)

    dk = dk_keep + swap_core(dk_other)
    low, token = queries((0, 1))
    dk = ring_sum(dk.reshape(4, 4, 4, 32, 128), functools.partial(along, True))
    dk, token = lax.optimization_barrier((dk, token))
    high, token = queries((2, 3), token)
    dk = ring_sum(dk, functools.partial(along, False))
    dk, token, low, high = lax.optimization_barrier((dk, token, low, high))
    dk = ring_sum(dk, lambda shift: lambda x, z, y, k: (x, z + shift, y, k))
    low, high = [v.reshape(2, 8, HALF, 128).transpose(0, 2, 1, 3).reshape(128, 8, 128) for v in (low, high)]
    query_grad = jnp.concatenate((low, high), axis=1)
    return query_grad, dk + token[0:1].astype(f32)


def solution(mesh):
    return jax.shard_map(
        per_device,
        mesh=mesh,
        in_specs=(
            P(),
            P("ctx", "head", None),
            P("ctx", None),
            P("ctx", "head"),
            P("ctx", "head", None),
            P("ctx", None),
            P("ctx", "head"),
        ),
        out_specs=(P("ctx", "head", None), P(("ctx", "head"), None)),
        check_vma=False,
    )
```

```python
import functools
import math

import jax
import jax.numpy as jnp
from jax import lax
from jax.experimental import pallas as pl
from jax.experimental.pallas import tpu as pltpu
from jax.sharding import PartitionSpec as P

ALL = ("ctx", "head")
HALF = 64
TILE = 256
PER_TILE = TILE // HALF
TILES = 17
LISTS = ((0, 16), (32, 64), (96, 112))
UNUSED = 32 * 4
SLOT, GOAL, ROW, ROW_OTHER, POSITION, COUNT = 0, 256, 512, 576, 640, 704
MLA_SCALE = 192.0**-0.5
LOSS_SCALE = 64.0
NT = (((1,), (1,)), ((), ()))
NN = (((1,), (0,)), ((), ()))


def permutation(move):
    pairs = []
    for x in range(4):
        for zl in range(2):
            for y in range(4):
                for zh in range(2):
                    for k in range(2):
                        tx, tz, ty, tk = move(x, 2 * zh + zl, y, k)
                        tx, tz, ty, tk = tx % 4, tz % 4, ty % 4, tk % 2
                        source = (x * 8 + zl * 4 + y) * 4 + zh * 2 + k
                        target = (tx * 8 + (tz % 2) * 4 + ty) * 4 + (tz // 2) * 2 + tk
                        pairs.append((source, target))
    return pairs


def send(value, move):
    return lax.ppermute(value, ALL, permutation(move))


def swap_core(value):
    return send(value, lambda x, z, y, k: (x, z, y, k + 1))


def swap_high(value):
    return send(value, lambda x, z, y, k: (x, z + 2, y, k))


def along(first, shift):
    def move(x, z, y, k):
        if (k == 0) == first:
            return (x, z, y + shift, k)
        return (x + shift, z, y, k)

    return move


def vmem():
    return pl.BlockSpec(memory_space=pltpu.VMEM)


def smem():
    return pl.BlockSpec(memory_space=pltpu.SMEM)


def anywhere():
    return pl.BlockSpec(memory_space=pl.ANY)


def params(mib):
    return pltpu.CompilerParams(vmem_limit_bytes=mib * 1024 * 1024)


def place(meta, step):
    half = (step >= meta[0]).astype(jnp.int32)
    return half, step - half * meta[0]


def plan_kernel(meta, order, slot, row, row_other, _after, plan):
    base = PER_TILE * meta[0]

    def step(i, ends):
        position, at = order[i], slot[i]
        plan[ROW + position] = row[i]
        plan[ROW_OTHER + position] = row_other[i]
        plan[POSITION + at] = position
        ring = (at // 8) % 4
        stage = jnp.where(ring == 0, 0, jnp.where(ring == 3, 2, 1))
        later = []
        for half in range(2):
            mine = ends[3 * half : 3 * half + 3]
            seen = jnp.where(position <= meta[2 + half], 1, 0)
            to = jnp.where(stage == 0, mine[0], jnp.where(stage == 1, mine[1], mine[2]))
            to = jnp.where(seen == 1, to, UNUSED)
            plan[SLOT + to] = at
            plan[GOAL + to] = position + base * half
            later += [end + jnp.where(stage == part, seen, 0) for part, end in enumerate(mine)]
        return tuple(later)

    ends = tuple(jnp.int32(LISTS[part][half]) for half in range(2) for part in range(3))
    ends = lax.fori_loop(0, 64, step, ends, unroll=8)
    for half in range(2):
        for part in range(3):
            end = ends[3 * half + part]
            tiles = (end - LISTS[part][half] + 3) // 4
            plan[COUNT + 3 * half + part] = tiles
            for u in range(3):
                to = jnp.where(end + u < LISTS[part][half] + 4 * tiles, end + u, UNUSED)
                plan[SLOT + to] = (0, 8, 24)[part]
                plan[GOAL + to] = 68


def pack(q_ref, n_ref, out):
    n = n_ref[...] * -math.sqrt(192.0)
    n1 = n.astype(jnp.bfloat16).astype(jnp.float32)
    n2 = (n - n1).astype(jnp.bfloat16).astype(jnp.float32)
    n3 = n - n1 - n2
    row = lax.broadcasted_iota(jnp.int32, (64, 128), 0)
    for i in range(16):
        lanes = slice(i * 128, (i + 1) * 128)
        a, b = q_ref[2 * i], q_ref[2 * i + 1]
        out[0, 0:576, lanes] = jnp.concatenate((a[:, 0:64], b[:, 0:64]), axis=1)
        out[1, 0:576, lanes] = jnp.concatenate((a[:, 64:128], b[:, 64:128]), axis=1)
        for half in range(2):
            cut = slice(half * 64, half * 64 + 64)
            parts = [
                jnp.concatenate((v[2 * i : 2 * i + 1, cut], v[2 * i + 1 : 2 * i + 2, cut]), axis=1)
                for v in (n1, n2, n3)
            ]
            block = jnp.where(row == 0, parts[0], jnp.where(row == 1, parts[1], jnp.where(row == 2, parts[2], 0.0)))
            out[half, 576:640, lanes] = block.astype(jnp.bfloat16)


def target_kernel(stage, unread, meta, plan, q_ref, *refs):
    count, size, base = ((1, 8, 0), (2, 8, 8), (2, 4, 24))[stage]
    groups, refs = (refs[0:count], refs[count : 2 * count]), refs[2 * count :]
    n_ref, keys, sems = refs[0], refs[-2], refs[-1]
    refs = refs[(2 if stage else 1) + unread : -2]
    if stage == 0:
        sums, sorted_ref, token, packed = refs
    elif stage == 1:
        sums, sorted_ref, token = refs
    else:
        sums, sorted_ref, keep, other = refs
    if stage < 2:
        token[...] = jnp.zeros(token.shape, jnp.int32)
    core = meta[1]
    copies = []
    for side, group in enumerate(groups):
        owner = core if side == 0 else 1 - core
        for j, ref in enumerate(group):
            at = owner * 32 + base + j * size
            copies.append(pltpu.make_async_copy(ref, keys.at[pl.ds(at, size)], sems.at[side * count + j]))
    for copy in copies:
        copy.start()
    if stage == 0:
        pack(q_ref, n_ref, packed)
        q_ref = packed
    for copy in copies:
        copy.wait()
    for owner in range(2):

        def sort(i, _, owner=owner):
            slot = owner * 32 + i
            at = pl.multiple_of(plan[POSITION + slot] * HALF, HALF)
            sorted_ref[pl.ds(at, HALF), :] = keys[slot, :, 640:768]
            return 0

        lax.fori_loop(base, base + count * size, sort, 0, unroll=4)
    scale = MLA_SCALE * math.log2(math.e)
    first = plan[COUNT + stage]
    tiles = first + plan[COUNT + 3 + stage]

    def body(t):
        half = jnp.where(t >= first, 1, 0)
        at = LISTS[stage][0] + t * PER_TILE + half * (LISTS[stage][1] - LISTS[stage][0] - first * PER_TILE)
        tile = jnp.concatenate([keys[plan[SLOT + at + u], :, 0:640] for u in range(PER_TILE)], axis=0)
        total = jnp.zeros((TILE, 128), jnp.float32)
        for g in range(8):
            s = lax.dot_general(
                tile, q_ref[half, :, g * 256 : (g + 1) * 256], NN, preferred_element_type=jnp.float32
            )
            e = jnp.exp2(s * scale)
            total = total + (e[:, 0:128] + e[:, 128:256])
        for u in range(PER_TILE):
            sums[plan[GOAL + at + u]] = total[u * HALF : (u + 1) * HALF]

    def pair(i, _):
        body(2 * i)
        body(2 * i + 1)
        return 0

    lax.fori_loop(0, tiles // 2, pair, 0)

    @pl.when(tiles % 2 == 1)
    def _():
        body(tiles - 1)

    if stage == 2:

        def fold(step, _):
            total = sums[pl.ds(step * PER_TILE, PER_TILE)].reshape(TILE, 128).T
            total = total[0:64] + total[64:128]
            top, low = total[0:32], total[32:64]
            keep[step] = jnp.where(core == 0, top, low)
            other[step] = jnp.where(core == 0, low, top)
            return 0

        lax.fori_loop(0, TILES, fold, 0, unroll=4)


def take_kernel(start, source, out, sem):
    copy = pltpu.make_async_copy(source.at[pl.ds(start, 4)], out, sem)
    copy.start()
    copy.wait()


def visible_of(meta, half, ktile):
    rows = lax.broadcasted_iota(jnp.int32, (32, TILE), 0) + meta[1] * 32 + meta[2 + half] * HALF
    cols = lax.broadcasted_iota(jnp.int32, (32, TILE), 1) + ktile * TILE
    return cols <= rows


def logit_kernel(idx_scale, meta, a_ref, b_ref, key_ref, iq_ref, out, scaled, iqt, wide, top, norm):
    for half in range(2):
        iqt[half] = iq_ref[half, 0:16].reshape(1024, 128).T
    spread(iq_ref, scaled, idx_scale)
    for side, ref in enumerate((a_ref, b_ref)):
        for c in range(2):
            for half in range(2):
                w = ref[c, half, 16].astype(jnp.float32)
                for j in range(16):
                    wide[side, c, half, pl.ds(j * 32, 32)] = jnp.broadcast_to(w[:, j : j + 1], (32, 128))
    top[...] = jnp.full(top.shape, -jnp.inf, jnp.float32)
    norm[...] = jnp.zeros(norm.shape, jnp.float32)

    def first(step, _):
        half, ktile = place(meta, step)
        tile = key_ref[pl.ds(pl.multiple_of(ktile * TILE, TILE), TILE), :]
        total = jnp.zeros((32, TILE), jnp.float32)
        for side, ref in enumerate((a_ref, b_ref)):
            for c in range(2):
                rows = ref[c, half, 0:16].reshape(512, 128)
                d = jnp.maximum(lax.dot_general(rows, tile, NT, preferred_element_type=jnp.float32), 0.0)
                w = wide[side, c, half]
                d = d * jnp.concatenate((w, w), axis=1)
                for j in range(16):
                    total = total + d[j * 32 : (j + 1) * 32]
        logits = jnp.where(visible_of(meta, half, ktile), total * idx_scale, -jnp.inf)
        out[step] = logits
        top[half] = jnp.maximum(top[half], logits)
        return 0

    lax.fori_loop(0, TILES, first, 0, unroll=4)
    for half in range(2):
        top[half] = jnp.broadcast_to(jnp.max(top[half], axis=1, keepdims=True), (32, TILE))

    def second(step, _):
        half, _ktile = place(meta, step)
        e = jnp.exp(out[step] - top[half])
        out[step] = e
        norm[half] = norm[half] + e
        return 0

    lax.fori_loop(0, TILES, second, 0)
    for half in range(2):
        norm[half] = jnp.broadcast_to(1.0 / jnp.sum(norm[half], axis=1, keepdims=True), (32, TILE))

    def third(step, _):
        half, _ktile = place(meta, step)
        out[step] = out[step] * norm[half]
        return 0

    lax.fori_loop(0, TILES, third, 0)


def gradient_kernel(meta, p_ref, a_ref, b_ref, c_ref, out, whole, total):
    total[...] = jnp.zeros(total.shape, jnp.float32)

    def first(step, _):
        half, ktile = place(meta, step)
        t = a_ref[step] + b_ref[step] + c_ref[step].astype(jnp.float32)
        t = jnp.where(visible_of(meta, half, ktile), t, 0.0)
        whole[step] = t
        total[half] = total[half] + t
        return 0

    lax.fori_loop(0, TILES, first, 0)
    for half in range(2):
        total[half] = jnp.broadcast_to(1.0 / jnp.sum(total[half], axis=1, keepdims=True), (32, TILE))

    def second(step, _):
        half, _ktile = place(meta, step)
        out[step] = (LOSS_SCALE * (p_ref[step] - whole[step] * total[half])).astype(jnp.bfloat16)
        return 0

    lax.fori_loop(0, TILES, second, 0)


def spread(iq_ref, wide, idx_scale):
    for half in range(2):
        w = iq_ref[half, 16].astype(jnp.float32) * idx_scale
        for j in range(16):
            wide[half, pl.ds(j * HALF, HALF)] = jnp.broadcast_to(w[:, j : j + 1], (HALF, 128))


def coefficients(meta, step, g_ref, h_ref, iq_ref, key_ref, wide, groups=(0, 1, 2, 3)):
    core = meta[1]
    half, ktile = place(meta, step)
    tile = key_ref[pl.ds(pl.multiple_of(ktile * TILE, TILE), TILE), :]
    mine, theirs = g_ref[step].astype(jnp.float32), h_ref[step].astype(jnp.float32)
    g = jnp.concatenate((jnp.where(core == 0, mine, theirs), jnp.where(core == 0, theirs, mine)), axis=0)
    g = jnp.concatenate((g, g, g, g), axis=0)
    found = []
    for q in groups:
        rows = iq_ref[half, pl.ds(q * 4, 4)].reshape(256, 128)
        d = lax.dot_general(rows, tile, NT, preferred_element_type=jnp.float32)
        w = wide[half, pl.ds(q * 256, 256)]
        found.append(jnp.where(d > 0, g * jnp.concatenate((w, w), axis=1), 0.0).astype(jnp.bfloat16))
    return half, ktile, tile, found


def key_kernel(meta, plan, g_ref, h_ref, iq_ref, iqt_ref, key_ref, wide, keep, other):
    core = meta[1]
    keep[...] = jnp.zeros(keep.shape, jnp.float32)
    other[...] = jnp.zeros(other.shape, jnp.float32)

    def body(step, _):
        half, ktile, _tile, found = coefficients(meta, step, g_ref, h_ref, iq_ref, key_ref, wide)
        dkt = lax.dot_general(
            iqt_ref[half], jnp.concatenate(found, axis=0), NN, preferred_element_type=jnp.float32
        )
        dk = dkt.T
        for u in range(PER_TILE):
            slot, slot_other = plan[ROW + ktile * PER_TILE + u], plan[ROW_OTHER + ktile * PER_TILE + u]
            first, last = dk[u * 64 : u * 64 + 32], dk[u * 64 + 32 : u * 64 + 64]
            keep[slot] = keep[slot] + jnp.where(core == 0, first, last)
            other[slot_other] = other[slot_other] + jnp.where(core == 0, last, first)
        return 0

    lax.fori_loop(0, TILES, body, 0, unroll=4)


def query_kernel(groups, meta, g_ref, h_ref, iq_ref, key_ref, wide, *refs):
    dq, token = refs[-2:]
    token[...] = jnp.zeros(token.shape, jnp.int32)
    dq[...] = jnp.zeros(dq.shape, jnp.float32)

    def body(step, _):
        half, _ktile, tile, found = coefficients(meta, step, g_ref, h_ref, iq_ref, key_ref, wide, groups)
        for q in range(4):
            dq[half, pl.ds(q * 256, 256)] = dq[half, pl.ds(q * 256, 256)] + lax.dot_general(
                found[q], tile, NN, preferred_element_type=jnp.float32
            )
        return 0

    lax.fori_loop(0, TILES, body, 0, unroll=4)


def ring_sum(value, route):
    got = [send(value[shift], route(shift)) for shift in (1, 3, 2)]
    return value[0] + got[0] + got[1] + got[2]


def per_device(
    block_order, query_latent, key_latent, normalizer, indexer_query, indexer_key, indexer_weight
):
    f32, bf16 = jnp.float32, jnp.bfloat16
    idx_scale = 8192.0**-0.5
    ctx, head = lax.axis_index("ctx"), lax.axis_index("head")
    x, zl, y = ctx // 8, (ctx // 4) % 2, ctx % 4
    core = head % 2

    small = pl.CostEstimate(flops=1_000_000, bytes_accessed=1_000_000, transcendentals=0)
    flag = jax.ShapeDtypeStruct((8, 128), jnp.int32)
    part = jax.ShapeDtypeStruct((TILES, 32, TILE), f32)

    index = jnp.arange(64, dtype=jnp.int32)
    bc, bk = index // 2, index % 2
    bx, bz, by = bc // 8, (bc // 4) % 2, bc % 4

    def ring_slot(rel):
        return jnp.where(rel == 0, 0, jnp.where(rel == 3, 1, jnp.where(rel == 1, 2, 3)))

    rx, ry = ring_slot((bx - x) % 4), ring_slot((by - y) % 4)
    rz = (bz != zl).astype(jnp.int32)
    slot = bk * 32 + jnp.where(bk == 0, rx * 8 + ry * 2, ry * 8 + rx * 2) + rz
    blocks = lax.dynamic_slice_in_dim(block_order, ctx * 2, 2, 0)
    qx, qy = (bx - x) % 4, (by - y) % 4
    qz = (2 * bk + bz - 2 * (head // 2) - zl) % 4
    row_a, row_b = qy * 16 + qx * 4 + qz, qx * 16 + qy * 4 + qz
    row_a, row_b = jnp.where(core == 0, row_a, row_b), jnp.where(core == 0, row_b, row_a)
    meta = jnp.concatenate(((blocks[0:1] + PER_TILE) // PER_TILE, core[None], blocks)).astype(jnp.int32)
    ones = (lax.broadcasted_iota(jnp.int32, (128, 64), 1) < 3).astype(bf16)
    packed = jnp.concatenate((key_latent, ones, indexer_key), axis=1)
    own = lax.dynamic_slice_in_dim(packed, core * HALF, HALF, 0)
    beside = send(own, lambda x, z, y, k: (x, z + 1 - 2 * k, y, k))
    pair = jnp.stack((own, beside))
    plan = pl.pallas_call(
        plan_kernel,
        out_shape=jax.ShapeDtypeStruct((768,), jnp.int32),
        in_specs=[smem()] * 5 + [anywhere()],
        out_specs=smem(),
        compiler_params=params(1),
        cost_estimate=small,
        name="plan",
    )(meta, block_order, slot, row_a, row_b, pair)
    legs = [pair] + [send(pair, along(True, shift)) for shift in (1, 3, 2)]
    group = jnp.concatenate(legs, axis=0)
    iq = indexer_query.reshape(2, HALF, 16, 128).transpose(0, 2, 1, 3)
    weight = jnp.pad(indexer_weight.reshape(2, 1, HALF, 16), ((0, 0), (0, 0), (0, 0), (0, 112)))
    iqw = jnp.concatenate((iq, weight), axis=1)
    iq_high = swap_high(iqw)
    group, plan, iq_flag = lax.optimization_barrier((group, plan, iq_high[0, 0, 0:8]))
    iq_both = jnp.stack((iqw, iq_high))
    iq_keep = lax.dynamic_slice_in_dim(iq_both, core * 32, 32, 3)
    iq_send = lax.dynamic_slice_in_dim(iq_both, (1 - core) * 32, 32, 3)
    iq_other = swap_core(iq_send)

    def targets(stage, outs, after, *arrays):
        reads = (2, 4, 4)[stage]
        held = len(arrays) - 1 - reads
        return pl.pallas_call(
            functools.partial(target_kernel, stage, len(after)),
            out_shape=(jax.ShapeDtypeStruct((69, HALF, 128), f32), jax.ShapeDtypeStruct((4096, 128), bf16)) + outs,
            in_specs=[smem(), smem(), vmem()] + [anywhere()] * reads + [vmem()] * held + [anywhere()] * len(after),
            out_specs=(vmem(),) * (2 + len(outs)),
            scratch_shapes=[pltpu.VMEM((64, HALF, 768), bf16), pltpu.SemaphoreType.DMA((reads,))],
            input_output_aliases={3 + reads: 0, 4 + reads: 1} if stage else {},
            compiler_params=params(16),
            cost_estimate=small,
            name=("targets_first", "targets_near", "targets_far")[stage],
        )(meta, plan, *arrays, *after)

    def take(value, start, after):
        return pl.pallas_call(
            lambda source, _after, out, sem: take_kernel(start, source, out, sem),
            out_shape=jax.ShapeDtypeStruct((4, HALF, 768), bf16),
            in_specs=[anywhere(), anywhere()],
            out_specs=anywhere(),
            scratch_shapes=[pltpu.SemaphoreType.DMA],
            compiler_params=params(1),
            cost_estimate=small,
            name="take",
        )(value, after)

    up, down = send(group, along(False, 1)), send(group, along(False, 3))
    sums, sorted_keys, token, query = targets(
        0,
        (flag, jax.ShapeDtypeStruct((2, 640, 2048), bf16)),
        (iq_keep, iq_send),
        query_latent.transpose(1, 2, 0),
        group,
        swap_core(group),
        normalizer.T,
    )
    up, down, token = lax.optimization_barrier((up, down, token))
    far_a = send(take(up, 0, token), along(False, 1))
    far_b = send(take(down, 4, token), along(False, 3))
    near = (up, down, swap_core(up), swap_core(down))
    sums, sorted_keys, token = targets(1, (flag,), (token, iq_flag, iq_other), query, *near, sums, sorted_keys)
    far_a, far_b, token = lax.optimization_barrier((far_a, far_b, token))
    far = (far_a, far_b, swap_core(far_a), swap_core(far_b))
    _, sorted_keys, keep, other = targets(2, (part, part), (token,), query, *far, sums, sorted_keys)
    from_core = swap_core(other)
    from_high = swap_high((keep + from_core).astype(bf16))

    prob, scaled, iqt = pl.pallas_call(
        functools.partial(logit_kernel, idx_scale),
        out_shape=(part, jax.ShapeDtypeStruct((2, 1024, 128), f32), jax.ShapeDtypeStruct((2, 128, 1024), bf16)),
        in_specs=[smem()] + [vmem()] * 4,
        out_specs=(vmem(), vmem(), vmem()),
        scratch_shapes=[
            pltpu.VMEM((2, 2, 2, 512, 128), f32),
            pltpu.VMEM((2, 32, TILE), f32),
            pltpu.VMEM((2, 32, TILE), f32),
        ],
        compiler_params=params(12),
        cost_estimate=small,
        name="logits",
    )(meta, iq_keep, iq_other, sorted_keys, iqw)

    grad = pl.pallas_call(
        gradient_kernel,
        out_shape=jax.ShapeDtypeStruct((TILES, 32, TILE), bf16),
        in_specs=[smem()] + [vmem()] * 4,
        out_specs=vmem(),
        scratch_shapes=[pltpu.VMEM((TILES, 32, TILE), f32), pltpu.VMEM((2, 32, TILE), f32)],
        compiler_params=params(8),
        cost_estimate=small,
        name="gradient",
    )(meta, prob, keep, from_core, from_high)
    grad_other = swap_core(grad)

    shard = jax.ShapeDtypeStruct((64, 32, 128), f32)
    dk_keep, dk_other = pl.pallas_call(
        key_kernel,
        out_shape=(shard, shard),
        in_specs=[smem(), smem()] + [vmem()] * 6,
        out_specs=(vmem(), vmem()),
        compiler_params=params(12),
        cost_estimate=small,
        name="keys",
    )(meta, plan, grad, grad_other, iqw, iqt, sorted_keys, scaled)
    def queries(groups, *after):
        return pl.pallas_call(
            functools.partial(query_kernel, groups),
            out_shape=(jax.ShapeDtypeStruct((2, 1024, 128), f32), flag),
            in_specs=[smem()] + [vmem()] * 5 + [anywhere()] * len(after),
            out_specs=(vmem(), vmem()),
            compiler_params=params(12),
            cost_estimate=small,
            name="queries",
        )(meta, grad, grad_other, iqw, sorted_keys, scaled, *after)

    dk = dk_keep + swap_core(dk_other)
    dq, token = queries((0, 1, 2, 3))
    dk = ring_sum(dk.reshape(4, 4, 4, 32, 128), functools.partial(along, True))
    dk, token = lax.optimization_barrier((dk, token))
    dk = ring_sum(dk, functools.partial(along, False))
    dk, dq = lax.optimization_barrier((dk, dq))
    dk = ring_sum(dk, lambda shift: lambda x, z, y, k: (x, z + shift, y, k))
    query_grad = dq.reshape(2, 16, HALF, 128).transpose(0, 2, 1, 3).reshape(128, 16, 128)
    return query_grad, dk + token[0:1].astype(f32)


def solution(mesh):
    return jax.shard_map(
        per_device,
        mesh=mesh,
        in_specs=(
            P(),
            P("ctx", "head", None),
            P("ctx", None),
            P("ctx", "head"),
            P("ctx", "head", None),
            P("ctx", None),
            P("ctx", "head"),
        ),
        out_specs=(P("ctx", "head", None), P(("ctx", "head"), None)),
        check_vma=False,
    )
```
